32 devices in a mesh: row: 8 (over z, x), col: 2 (over y), seq: 2 (over core).
Axes of the slice: x: 2, y: 2, z: 4, core: 2. Of those that a mesh axis runs over, the one named last changes fastest.
Arguments:
- out_grads: bfloat16 [1, 2048, 32768], P(None, 'seq', 'row'), may hold values from -0.125 to 0.125
- layer_inputs: bfloat16 [1, 2048, 8192], P(None, 'seq', 'col'), may hold values from -6 to 6
- row_bits: int32 [32768], P('row'), may hold values from 0 to 1
- col_bits: int32 [8192], P('col'), may hold values from 0 to 1
- row_blocks: int32 [16], replicated, may hold values from 0 to 511
- col_blocks: int32 [8], replicated, may hold values from 0 to 63
Outputs:
- sketch: float32 [1, 1024, 1024], P(None, 'row', 'col')
The draws below stay inside these ranges and needn't reach their ends.
Inputs may be any that keep to these rules, and one draw needn't show every extreme that they name: `row_blocks`: blocks may repeat. `col_blocks`: blocks may repeat.
All inputs are finite; a program needn't handle non-finite values.
Results may differ from the reference program's by a relative error of at most 0.0003.
Values sent between devices are 32-bit elements; how exact they have to be, the bound alone decides.
No kernel may reach another device: no remote copies, remote signals or barrier semaphores. Data moves between devices by JAX's collectives and lax.ppermute only.
A program may use at most 128 MiB of HBM per device.

```python
import math
import jax
import jax.numpy as jnp
from jax import lax

D = 8192
FF = 28672
FFP = 32768
EX = 1
TOKENS = 2048
BR = 64
KR = 16
BC = 128
KC = 8


def touch_ends(entries, stream_key, smallest, largest):
    extent = entries.shape
    index_at = [jax.random.randint(jax.random.fold_in(stream_key, axis), (), 0, extent[axis]) for axis in range(len(extent))]
    entries = entries.at[tuple(index_at)].set(smallest)
    longest = extent.index(max(extent))
    index_at[longest] = (index_at[longest] + 1) % extent[longest]
    return entries.at[tuple(index_at)].set(largest)


def shard_levels(stream_key, shape, split, least, top_value):
    factor_of, own = 1.0, jax.random.fold_in(stream_key, 6)
    for axis_at, blocks in split:
        steps = jnp.exp(jax.random.uniform(jax.random.fold_in(own, axis_at), (blocks,), jnp.float32, least / len(split), top_value / len(split)))
        factor_of = factor_of * jnp.repeat(steps, shape[axis_at] // blocks).reshape([-1 if axis == axis_at else 1 for axis in range(len(shape))])
    return factor_of


def gaussian(own_key, shape, spread, most, pieces=(), kind=jnp.bfloat16):
    array = spread * jax.random.normal(own_key, shape, jnp.float32)
    if pieces:
        array = array * shard_levels(own_key, shape, pieces, -0.22, 0.18)
    return jnp.clip(array, -most, most).astype(kind)


def setup_inputs(seed: int = 0) -> dict:
    splits = jax.random.split(jax.random.key(seed), 7)
    out_grads = gaussian(splits[0], (EX, TOKENS, FFP), (TOKENS ** -0.5), 0.125, ((1, 2), (2, 8)))
    layer_inputs = gaussian(splits[1], (EX, TOKENS, D), 1.0, 6.0, ((1, 2), (2, 2)))
    row_bits = touch_ends(jax.random.randint(splits[2], (FFP,), 0, 2), jax.random.fold_in(splits[2], 1), 0, 1).astype(jnp.int32)
    col_bits = touch_ends(jax.random.randint(splits[3], (D,), 0, 2), jax.random.fold_in(splits[3], 1), 0, 1).astype(jnp.int32)
    row_blocks = touch_ends(jax.random.randint(splits[4], (KR,), 0, FFP // BR), jax.random.fold_in(splits[4], 1), 0, (FFP // BR) - 1).astype(jnp.int32)
    col_blocks = touch_ends(jax.random.randint(splits[5], (KC,), 0, D // BC), jax.random.fold_in(splits[5], 1), 0, (D // BC) - 1).astype(jnp.int32)
    return {"out_grads": out_grads, "layer_inputs": layer_inputs, "row_bits": row_bits, "col_bits": col_bits, "row_blocks": row_blocks, "col_blocks": col_blocks}


def parity_sign(first, second):
    joined = jnp.bitwise_and(first, second)
    parity = jnp.zeros(joined.shape, jnp.int32)
    for position in range(16):
        parity = parity + jnp.bitwise_and(jnp.right_shift(joined, position), 1)
    return (1 - 2 * (parity % 2)).astype(jnp.float32)

def hadamard_table(order):
    index = jnp.arange(order, dtype=jnp.int32)
    return parity_sign(index[:, None], index[None, :])

def mix_last(values):
    length = values.shape[-1]
    batch = math.prod(values.shape[:-1])
    mixing = values.reshape(batch, length)
    before = 1
    remaining = length
    while remaining > 1:
        factor = min(64, remaining)
        after = remaining // factor
        table = hadamard_table(factor)
        mixing = jnp.einsum('ij,bpjq->bpiq', table, mixing.reshape(batch, before, factor, after), precision=lax.Precision.HIGHEST)
        before = before * factor
        remaining = after
    return mixing.reshape(values.shape)

def reference(out_grads, layer_inputs, row_bits, col_bits, row_blocks, col_blocks):
    row_sign = (1 - 2 * row_bits).astype(jnp.float32) * (jnp.arange(FFP, dtype=jnp.int32) < FF).astype(jnp.float32)
    col_sign = (1 - 2 * col_bits).astype(jnp.float32)
    left = mix_last(out_grads.astype(jnp.float32) * row_sign)
    left = jnp.take(left.reshape(EX, TOKENS, FFP // BR, BR), row_blocks, axis=2).reshape(EX, TOKENS, KR * BR)
    right = mix_last(layer_inputs.astype(jnp.float32) * col_sign)
    right = jnp.take(right.reshape(EX, TOKENS, D // BC, BC), col_blocks, axis=2).reshape(EX, TOKENS, KC * BC)
    sketch = jnp.einsum('etk,etj->ekj', left, right, precision=lax.Precision.HIGHEST)
    return sketch / math.sqrt(FFP * D)
```

```python
import math

import jax
import jax.numpy as jnp
from jax import lax
from jax.sharding import PartitionSpec as P

FF = 28672
BR = 64
BC = 128


def parity_sign(first, second):
    joined = jnp.bitwise_and(first, second)
    for shift in (16, 8, 4, 2, 1):
        joined = jnp.bitwise_xor(joined, jnp.right_shift(joined, shift))
    return 1 - 2 * jnp.bitwise_and(joined, 1)


def split_pieces(values):
    high = lax.reduce_precision(values, 8, 7)
    low = values - high
    return high.astype(jnp.bfloat16), low.astype(jnp.bfloat16)


class Plan:
    def __init__(self, mesh, row_kept):
        self.rows, self.cols, self.seqs = mesh.shape["row"], mesh.shape["col"], mesh.shape["seq"]
        self.split = self.seqs if self.seqs == 2 and (row_kept // self.rows) % 2 == 0 else 1
        row_bits = [("row", 1 << bit) for bit in range(self.rows.bit_length() - 1)]
        col_bits = [("col", 1 << bit) for bit in range(self.cols.bit_length() - 1)]
        last = row_bits[-1:]
        early = col_bits + row_bits[:-1]
        turn = len(early) - 1 if early else 0
        first = early
        second = early[1:] + early[:1]
        third = early[turn:] + early[:turn]
        self.main = (first + last, second + last)
        self.rest = (third + last, third + last)

    def pairs(self, bits):
        found = []
        for row in range(self.rows):
            for col in range(self.cols):
                for seq in range(self.seqs):
                    axis, mask = bits[seq % 2]
                    other_row = row ^ mask if axis == "row" else row
                    other_col = col ^ mask if axis == "col" else col
                    found.append(
                        (
                            (row * self.cols + col) * self.seqs + seq,
                            (other_row * self.cols + other_col) * self.seqs + seq,
                        )
                    )
        return found

    def place(self, order, row, col):
        spot = 0
        for axis, mask in order:
            spot = spot * 2 + int(bool((row if axis == "row" else col) & mask))
        return spot

    def halve(self, part, orders, step):
        half = part.shape[0] // 2
        bits = (orders[0][step], orders[1][step])
        return part[:half] + lax.ppermute(part[half:], ("row", "col", "seq"), self.pairs(bits))


def body(plan, out_grads, layer_inputs, row_bits, col_bits, row_blocks, col_blocks):
    row_local = out_grads.shape[2]
    col_local = layer_inputs.shape[2]
    row_kept = row_blocks.shape[0]
    col_kept = col_blocks.shape[0]
    row_place = lax.axis_index("row")
    col_place = lax.axis_index("col")
    seq_place = lax.axis_index("seq")
    global_rows = row_place * row_local + jnp.arange(row_local, dtype=jnp.int32)
    global_cols = col_place * col_local + jnp.arange(col_local, dtype=jnp.int32)
    row_sign = (1 - 2 * row_bits) * (global_rows < FF).astype(jnp.int32)
    col_sign = 1 - 2 * col_bits
    scale = 1.0 / math.sqrt(row_local * plan.rows * col_local * plan.cols)

    per_row = row_kept // plan.rows
    per_col = col_kept // plan.cols
    rel_row = jnp.arange(plan.rows, dtype=jnp.int32) ^ row_place
    rel_col = jnp.arange(plan.cols, dtype=jnp.int32) ^ col_place
    inner = jnp.arange(per_row, dtype=jnp.int32)
    if plan.split == 2:
        inner = inner.reshape(per_row // 2, 2) ^ seq_place
        row_order = rel_row[None, :, None] * per_row + inner.T[:, None, :]
    else:
        row_order = rel_row[None, :, None] * per_row + inner[None, None, :]
    col_order = rel_col[:, None] * per_col + jnp.arange(per_col, dtype=jnp.int32)[None, :]
    row_want = (jnp.take(row_blocks, row_order.reshape(-1))[:, None] * BR + jnp.arange(BR)[None, :]).reshape(-1)
    col_want = (jnp.take(col_blocks, col_order.reshape(-1))[:, None] * BC + jnp.arange(BC)[None, :]).reshape(-1)
    row_table = (parity_sign(global_rows[:, None], row_want[None, :]) * row_sign[:, None]).astype(jnp.bfloat16)
    col_table = (parity_sign(global_cols[:, None], col_want[None, :]) * col_sign[:, None]).astype(jnp.bfloat16)
    left = jnp.dot(out_grads[0], row_table, preferred_element_type=jnp.float32)
    right = jnp.dot(layer_inputs[0], col_table, preferred_element_type=jnp.float32)
    left_high, left_low = split_pieces(left * scale)
    right_high, right_low = split_pieces(right)

    def product(first, second):
        return lax.dot_general(first, second, (((0,), (0,)), ((), ())), preferred_element_type=jnp.float32)

    whole = (
        product(left_high, right_high) + product(left_high, right_low) + product(left_low, right_high)
    )
    rows_each = row_kept * BR // plan.rows // plan.split
    cols_each = col_kept * BC // plan.cols
    whole = whole.reshape(plan.split, plan.rows, rows_each, plan.cols, cols_each)
    whole = whole.transpose(0, 1, 3, 2, 4).reshape(plan.split, plan.rows * plan.cols, rows_each, cols_each)

    def arranged(orders):
        tables = []
        for order in orders:
            table = [0] * (plan.rows * plan.cols)
            for row in range(plan.rows):
                for col in range(plan.cols):
                    table[plan.place(order, row, col)] = row * plan.cols + col
            tables.append(table)
        return jnp.take(jnp.array(tables, dtype=jnp.int32), seq_place % 2, axis=0)

    cut = rows_each * 3 // 4
    whole = [whole[part] for part in range(plan.split)]
    main = [jnp.take(part[:, :cut], arranged(plan.main[at:] + plan.main[:at]), axis=0) for at, part in enumerate(whole)]
    rest = [jnp.take(part[:, cut:], arranged(plan.rest), axis=0) for part in whole]
    if plan.split == 2:
        swap = [(0, 1), (1, 0)]
        main = main[0] + lax.ppermute(main[1], "seq", swap)
        rest = rest[0] + lax.ppermute(rest[1], "seq", swap)
    else:
        main, rest = main[0], rest[0]
    steps = len(plan.main[0])
    for step in range(steps - 1):
        main = plan.halve(main, plan.main, step)
        rest = plan.halve(rest, plan.rest, step)
    both = plan.halve(jnp.concatenate([main, rest], axis=1), plan.rest, steps - 1)[0]
    if plan.split == 2:
        both = lax.all_gather(both, "seq", axis=0)
        both = both.reshape(2, per_row // 2, BR, cols_each).transpose(1, 0, 2, 3)
        return both.reshape(1, per_row * BR, cols_each)
    return lax.psum(both, "seq")[None]


def solution(mesh):
    def run(out_grads, layer_inputs, row_bits, col_bits, row_blocks, col_blocks):
        plan = Plan(mesh, row_blocks.shape[0])
        in_specs = (P(None, "seq", "row"), P(None, "seq", "col"), P("row"), P("col"), P(), P())
        return jax.shard_map(
            lambda *args: body(plan, *args),
            mesh=mesh,
            in_specs=in_specs,
            out_specs=P(None, "row", "col"),
            check_vma=False,
        )(out_grads, layer_inputs, row_bits, col_bits, row_blocks, col_blocks)

    return run
```

```python
import functools
import math

import jax
import jax.numpy as jnp
import numpy as np
from jax import lax
from jax.experimental import pallas as pl
from jax.experimental.pallas import tpu as pltpu
from jax.sharding import PartitionSpec as P

FF = 28672
BR = 64
BC = 128
CHUNK = 256
TILE = 256
VMEM_LIMIT = 56 << 20


def scalar_parity(first, second):
    joined = first & second
    for shift in (8, 4, 2, 1):
        joined = joined ^ (joined >> shift)
    return joined & 1


def hadamard_table(order):
    index = np.arange(order)
    joined = index[:, None] & index[None, :]
    parity = sum((joined >> position) & 1 for position in range(order.bit_length()))
    return jnp.asarray(1 - 2 * (parity % 2), dtype=jnp.bfloat16)


def mix_group(parts):
    first, second = parts[0] + parts[1], parts[0] - parts[1]
    third, fourth = parts[2] + parts[3], parts[2] - parts[3]
    return first + third, second + fourth, first - third, second - fourth


def kept_sum(source, slot, sign, width, length, axis):
    per_chunk = CHUNK // width
    inside = slot % per_chunk
    chunk = slot // per_chunk
    low, high = chunk % 4, chunk // 4
    start = pl.multiple_of(inside * width, width)
    total = None
    for group in range(source.shape[0] // 4):
        weight = sign * (1 - 2 * scalar_parity(high, jnp.int32(group))).astype(jnp.float32)
        if axis == 0:
            piece = source[4 * group + low, pl.ds(start, width), :]
        else:
            piece = source[4 * group + low, :, pl.ds(start, width)]
        total = piece * weight if total is None else total + piece * weight
    return total


def store_pieces(values, high_ref, low_ref, where):
    high = values.astype(jnp.bfloat16)
    high_ref[where] = high
    low_ref[where] = (values - high.astype(jnp.float32)).astype(jnp.bfloat16)


def product_blocks(plan, here, left_high, left_low, right_high, right_low, out_ref, first_row, orders):
    rows, width = out_ref.shape[1], out_ref.shape[2]
    tile = min(CHUNK, width)
    span = pl.ds(first_row, plan.rows * rows)
    seq = here[2] % 2
    for start in range(0, plan.cols * width, tile):
        lanes = pl.ds(start, tile)
        total = jnp.dot(left_high[span, :], right_high[:, lanes], preferred_element_type=jnp.float32)
        total += jnp.dot(left_high[span, :], right_low[:, lanes], preferred_element_type=jnp.float32)
        total += jnp.dot(left_low[span, :], right_high[:, lanes], preferred_element_type=jnp.float32)
        col = start // width
        for row in range(plan.rows):
            places = [plan.place(order, row, col) for order in orders]
            place = jnp.where(seq == 0, places[0], places[1]) if places[0] != places[1] else places[0]
            out_ref[place, :, pl.ds(start % width, tile)] = total[row * rows : (row + 1) * rows, :]


def mix_kernel(
    plan, scale, here, row_blocks, col_blocks, grads, inputs, row_bits, col_bits, table,
    out, left_high, left_low, right_high, right_low, row_mixed, col_mixed,
):
    step = pl.program_id(0)
    tokens, row_local = grads.shape
    col_local = inputs.shape[1]
    mixing = table[...]
    index = lax.broadcasted_iota(jnp.int32, (1, row_local), 1) + here[0] * row_local
    row_sign = jnp.where(index < FF, 1 - 2 * row_bits[...], 0).astype(jnp.float32).astype(jnp.bfloat16)
    col_sign = (1 - 2 * col_bits[...]).astype(jnp.float32).astype(jnp.bfloat16)

    for group in range(row_local // CHUNK // 4):
        parts = []
        for chunk in range(4 * group, 4 * group + 4):
            lanes = slice(chunk * CHUNK, (chunk + 1) * CHUNK)
            signed = grads[:, lanes] * row_sign[:, lanes]
            parts.append(
                lax.dot_general(mixing, signed, (((1,), (1,)), ((), ())), preferred_element_type=jnp.float32)
            )
        for at, part in enumerate(mix_group(parts)):
            row_mixed[4 * group + at] = part
    for group in range(col_local // CHUNK // 4):
        parts = []
        for chunk in range(4 * group, 4 * group + 4):
            lanes = slice(chunk * CHUNK, (chunk + 1) * CHUNK)
            signed = inputs[:, lanes] * col_sign[:, lanes]
            parts.append(jnp.dot(signed, mixing, preferred_element_type=jnp.float32))
        for at, part in enumerate(mix_group(parts)):
            col_mixed[4 * group + at] = part

    now = pl.ds(pl.multiple_of(step * tokens, tokens), tokens)
    row_slots = row_local // BR
    inner = plan.per_row // plan.split
    cut = BR * 3 // 4
    for part in range(plan.split):
        base = part * plan.rows * inner * BR
        for row in range(plan.rows):
            for at in range(inner):
                kept = (here[0] ^ row) * plan.per_row + at * plan.split
                if plan.split == 2:
                    kept = kept + (here[2] ^ part)
                block = row_blocks[kept]
                sign = (1 - 2 * scalar_parity(block // row_slots, here[0])).astype(jnp.float32) * scale
                values = kept_sum(row_mixed, block % row_slots, sign, BR, tokens, 0)
                spot = row * inner + at
                first = base + spot * cut
                store_pieces(values[:cut], left_high, left_low, (pl.ds(first, cut), now))
                first = base + plan.rows * inner * cut + spot * (BR - cut)
                store_pieces(values[cut:], left_high, left_low, (pl.ds(first, BR - cut), now))
    col_slots = col_local // BC
    for col in range(plan.cols):
        for at in range(plan.per_col):
            block = col_blocks[(here[1] ^ col) * plan.per_col + at]
            sign = (1 - 2 * scalar_parity(block // col_slots, here[1])).astype(jnp.float32)
            values = kept_sum(col_mixed, block % col_slots, sign, BC, tokens, 1)
            store_pieces(values, right_high, right_low, (now, pl.ds((col * plan.per_col + at) * BC, BC)))

    @pl.when(step == pl.num_programs(0) - 1)
    def _():
        first, orders = plan.first_product()
        product_blocks(plan, here, left_high, left_low, right_high, right_low, out, first, orders)


def product_kernel(plan, wanted, here, left_high, left_low, right_high, right_low, *outs):
    for (first, orders), out in zip(wanted, outs):
        product_blocks(plan, here, left_high, left_low, right_high, right_low, out, first, orders)


class Plan:
    def __init__(self, mesh, row_kept, col_kept):
        self.rows, self.cols, self.seqs = mesh.shape["row"], mesh.shape["col"], mesh.shape["seq"]
        self.split = self.seqs if self.seqs == 2 and (row_kept // self.rows) % 2 == 0 else 1
        self.per_row = row_kept // self.rows
        self.per_col = col_kept // self.cols
        row_bits = [("row", 1 << bit) for bit in range(self.rows.bit_length() - 1)]
        col_bits = [("col", 1 << bit) for bit in range(self.cols.bit_length() - 1)]
        last = row_bits[-1:]
        early = col_bits + row_bits[:-1]
        turn = len(early) - 1 if early else 0
        first = early
        second = early[1:] + early[:1]
        third = early[turn:] + early[:turn]
        self.main = (first + last, second + last)
        self.rest = (third + last, third + last)

    def pairs(self, bits):
        found = []
        for row in range(self.rows):
            for col in range(self.cols):
                for seq in range(self.seqs):
                    axis, mask = bits[seq % 2]
                    other_row = row ^ mask if axis == "row" else row
                    other_col = col ^ mask if axis == "col" else col
                    found.append(
                        (
                            (row * self.cols + col) * self.seqs + seq,
                            (other_row * self.cols + other_col) * self.seqs + seq,
                        )
                    )
        return found

    def place(self, order, row, col):
        spot = 0
        for axis, mask in order:
            spot = spot * 2 + int(bool((row if axis == "row" else col) & mask))
        return spot

    def first_product(self):
        if self.split == 1:
            return 0, self.main
        return self.rows * self.per_row // 2 * BR, self.main[1:] + self.main[:1]

    def halve(self, part, orders, step):
        half = part.shape[0] // 2
        bits = (orders[0][step], orders[1][step])
        return part[:half] + lax.ppermute(part[half:], ("row", "col", "seq"), self.pairs(bits))


def body(plan, out_grads, layer_inputs, row_bits, col_bits, row_blocks, col_blocks):
    tokens, row_local = out_grads.shape[1:]
    col_local = layer_inputs.shape[2]
    tile = min(TILE, tokens)
    here = jnp.stack([lax.axis_index(name) for name in ("row", "col", "seq")]).astype(jnp.int32)
    scale = 1.0 / math.sqrt(row_local * plan.rows * col_local * plan.cols)
    left_rows = plan.rows * plan.per_row * BR
    right_cols = plan.cols * plan.per_col * BC
    inner = plan.per_row // plan.split
    cut = BR * 3 // 4
    cols_each = plan.per_col * BC
    blocks = plan.rows * plan.cols
    smem = pl.BlockSpec(memory_space=pltpu.SMEM)
    vmem = pl.BlockSpec(memory_space=pltpu.VMEM)
    main_shape = jax.ShapeDtypeStruct((blocks, inner * cut, cols_each), jnp.float32)
    rest_shape = jax.ShapeDtypeStruct((blocks, inner * (BR - cut), cols_each), jnp.float32)
    first_out, *factors = pl.pallas_call(
        functools.partial(mix_kernel, plan, scale),
        grid=(tokens // tile,),
        in_specs=[
            smem,
            smem,
            smem,
            pl.BlockSpec((tile, row_local), lambda step: (step, 0)),
            pl.BlockSpec((tile, col_local), lambda step: (step, 0)),
            vmem,
            vmem,
            vmem,
        ],
        out_specs=[vmem] * 5,
        out_shape=[
            main_shape,
            jax.ShapeDtypeStruct((left_rows, tokens), jnp.bfloat16),
            jax.ShapeDtypeStruct((left_rows, tokens), jnp.bfloat16),
            jax.ShapeDtypeStruct((tokens, right_cols), jnp.bfloat16),
            jax.ShapeDtypeStruct((tokens, right_cols), jnp.bfloat16),
        ],
        scratch_shapes=[
            pltpu.VMEM((row_local // CHUNK, CHUNK, tile), jnp.float32),
            pltpu.VMEM((col_local // CHUNK, tile, CHUNK), jnp.float32),
        ],
        compiler_params=pltpu.CompilerParams(vmem_limit_bytes=VMEM_LIMIT),
        name="mix",
    )(
        here,
        row_blocks,
        col_blocks,
        out_grads[0],
        layer_inputs[0],
        row_bits[None],
        col_bits[None],
        hadamard_table(CHUNK),
    )

    def products(wanted, shapes, name):
        return pl.pallas_call(
            functools.partial(product_kernel, plan, wanted),
            in_specs=[smem] + [vmem] * 4,
            out_specs=[vmem] * len(shapes),
            out_shape=shapes,
            compiler_params=pltpu.CompilerParams(vmem_limit_bytes=VMEM_LIMIT),
            name=name,
        )(here, *factors)

    swap = [(0, 1), (1, 0)]
    half_rows = plan.rows * inner * BR
    main_rows = plan.rows * inner * cut
    if plan.split == 2:
        arrived = lax.ppermute(first_out, "seq", swap)
        (mine,) = products([(0, plan.main)], [main_shape], "main_product")
        rest_mine, rest_other = products(
            [(main_rows, plan.rest), (half_rows + main_rows, plan.rest)], [rest_shape] * 2, "rest_products"
        )
        main = mine + arrived
        rest = rest_mine + lax.ppermute(rest_other, "seq", swap)
    else:
        main = first_out
        (rest,) = products([(main_rows, plan.rest)], [rest_shape], "rest_product")
    steps = len(plan.main[0])
    for step in range(steps - 1):
        main = plan.halve(main, plan.main, step)
        rest = plan.halve(rest, plan.rest, step)
    both = plan.halve(jnp.concatenate([main, rest], axis=1), plan.rest, steps - 1)[0]

    def in_rows(values):
        first = values[..., : inner * cut, :].reshape(*values.shape[:-2], inner, cut, cols_each)
        second = values[..., inner * cut :, :].reshape(*values.shape[:-2], inner, BR - cut, cols_each)
        return jnp.concatenate([first, second], axis=-2)

    if plan.split == 2:
        both = in_rows(lax.all_gather(both, "seq", axis=0))
        return both.transpose(1, 0, 2, 3).reshape(1, plan.per_row * BR, cols_each)
    return in_rows(lax.psum(both, "seq")).reshape(1, plan.per_row * BR, cols_each)


def solution(mesh):
    def run(out_grads, layer_inputs, row_bits, col_bits, row_blocks, col_blocks):
        plan = Plan(mesh, row_blocks.shape[0], col_blocks.shape[0])
        in_specs = (P(None, "seq", "row"), P(None, "seq", "col"), P("row"), P("col"), P(), P())
        return jax.shard_map(
            lambda *args: body(plan, *args),
            mesh=mesh,
            in_specs=in_specs,
            out_specs=P(None, "row", "col"),
            check_vma=False,
        )(out_grads, layer_inputs, row_bits, col_bits, row_blocks, col_blocks)

    return run
```

```python
import functools
import math

import jax
import jax.numpy as jnp
import numpy as np
from jax import lax
from jax.experimental import pallas as pl
from jax.experimental.pallas import tpu as pltpu
from jax.sharding import PartitionSpec as P

FF = 28672
BR = 64
BC = 128
CHUNK = 256
TILE = 256
MIX_VMEM = 30 << 20
PRODUCT_VMEM = 16 << 20


def scalar_parity(first, second):
    joined = first & second
    for shift in (8, 4, 2, 1):
        joined = joined ^ (joined >> shift)
    return joined & 1


def hadamard_table(order):
    index = np.arange(order)
    joined = index[:, None] & index[None, :]
    parity = sum((joined >> position) & 1 for position in range(order.bit_length()))
    return jnp.asarray(1 - 2 * (parity % 2), dtype=jnp.bfloat16)


def mix_group(parts):
    first, second = parts[0] + parts[1], parts[0] - parts[1]
    third, fourth = parts[2] + parts[3], parts[2] - parts[3]
    return first + third, second + fourth, first - third, second - fourth


def kept_sum(source, slot, sign, width, length, axis):
    per_chunk = CHUNK // width
    inside = slot % per_chunk
    chunk = slot // per_chunk
    low, high = chunk % 4, chunk // 4
    start = pl.multiple_of(inside * width, width)
    total = None
    for group in range(source.shape[0] // 4):
        weight = sign * (1 - 2 * scalar_parity(high, jnp.int32(group))).astype(jnp.float32)
        if axis == 0:
            piece = source[4 * group + low, pl.ds(start, width), :]
        else:
            piece = source[4 * group + low, :, pl.ds(start, width)]
        total = piece * weight if total is None else total + piece * weight
    return total


def store_pieces(values, high_ref, low_ref, where):
    high = values.astype(jnp.bfloat16)
    high_ref[where] = high
    low_ref[where] = (values - high.astype(jnp.float32)).astype(jnp.bfloat16)


def product_blocks(plan, here, left_high, left_low, right_high, right_low, out_ref, first_row, orders):
    rows, width = out_ref.shape[1], out_ref.shape[2]
    tile = min(CHUNK, width)
    span = pl.ds(first_row, plan.rows * rows)
    seq = here[2] % 2
    for start in range(0, plan.cols * width, tile):
        lanes = pl.ds(start, tile)
        total = jnp.dot(left_high[span, :], right_high[:, lanes], preferred_element_type=jnp.float32)
        total += jnp.dot(left_high[span, :], right_low[:, lanes], preferred_element_type=jnp.float32)
        total += jnp.dot(left_low[span, :], right_high[:, lanes], preferred_element_type=jnp.float32)
        col = start // width
        for row in range(plan.rows):
            places = [plan.place(order, row, col) for order in orders]
            place = jnp.where(seq == 0, places[0], places[1]) if places[0] != places[1] else places[0]
            out_ref[place, :, pl.ds(start % width, tile)] = total[row * rows : (row + 1) * rows, :]


def mix_kernel(
    plan, scale, here, row_blocks, col_blocks, grads, inputs, row_bits, col_bits, table,
    out, left_high, left_low, right_high, right_low, row_mixed, col_mixed,
):
    step = pl.program_id(0)
    tokens, row_local = grads.shape
    col_local = inputs.shape[1]
    mixing = table[...]
    index = lax.broadcasted_iota(jnp.int32, (1, row_local), 1) + here[0] * row_local
    row_sign = jnp.where(index < FF, 1 - 2 * row_bits[...], 0).astype(jnp.float32).astype(jnp.bfloat16)
    col_sign = (1 - 2 * col_bits[...]).astype(jnp.float32).astype(jnp.bfloat16)

    for group in range(row_local // CHUNK // 4):
        parts = []
        for chunk in range(4 * group, 4 * group + 4):
            lanes = slice(chunk * CHUNK, (chunk + 1) * CHUNK)
            signed = grads[:, lanes] * row_sign[:, lanes]
            parts.append(
                lax.dot_general(mixing, signed, (((1,), (1,)), ((), ())), preferred_element_type=jnp.float32)
            )
        for at, part in enumerate(mix_group(parts)):
            row_mixed[4 * group + at] = part
    for group in range(col_local // CHUNK // 4):
        parts = []
        for chunk in range(4 * group, 4 * group + 4):
            lanes = slice(chunk * CHUNK, (chunk + 1) * CHUNK)
            signed = inputs[:, lanes] * col_sign[:, lanes]
            parts.append(jnp.dot(signed, mixing, preferred_element_type=jnp.float32))
        for at, part in enumerate(mix_group(parts)):
            col_mixed[4 * group + at] = part

    now = pl.ds(pl.multiple_of(step * tokens, tokens), tokens)
    row_slots = row_local // BR
    inner = plan.per_row // plan.split
    cut = BR * 3 // 4
    for part in range(plan.split):
        base = part * plan.rows * inner * BR
        for row in range(plan.rows):
            for at in range(inner):
                kept = (here[0] ^ row) * plan.per_row + at * plan.split
                if plan.split == 2:
                    kept = kept + (here[2] ^ part)
                block = row_blocks[kept]
                sign = (1 - 2 * scalar_parity(block // row_slots, here[0])).astype(jnp.float32) * scale
                values = kept_sum(row_mixed, block % row_slots, sign, BR, tokens, 0)
                spot = row * inner + at
                first = base + spot * cut
                store_pieces(values[:cut], left_high, left_low, (pl.ds(first, cut), now))
                first = base + plan.rows * inner * cut + spot * (BR - cut)
                store_pieces(values[cut:], left_high, left_low, (pl.ds(first, BR - cut), now))
    col_slots = col_local // BC
    for col in range(plan.cols):
        for at in range(plan.per_col):
            block = col_blocks[(here[1] ^ col) * plan.per_col + at]
            sign = (1 - 2 * scalar_parity(block // col_slots, here[1])).astype(jnp.float32)
            values = kept_sum(col_mixed, block % col_slots, sign, BC, tokens, 1)
            store_pieces(values, right_high, right_low, (now, pl.ds((col * plan.per_col + at) * BC, BC)))

    @pl.when(step == pl.num_programs(0) - 1)
    def _():
        first, orders = plan.first_product()
        product_blocks(plan, here, left_high, left_low, right_high, right_low, out, first, orders)


def product_kernel(plan, wanted, here, left_high, left_low, right_high, right_low, *outs):
    for (first, orders), out in zip(wanted, outs):
        product_blocks(plan, here, left_high, left_low, right_high, right_low, out, first, orders)


class Plan:
    def __init__(self, mesh, row_kept, col_kept):
        self.rows, self.cols, self.seqs = mesh.shape["row"], mesh.shape["col"], mesh.shape["seq"]
        self.split = self.seqs if self.seqs == 2 and (row_kept // self.rows) % 2 == 0 else 1
        self.per_row = row_kept // self.rows
        self.per_col = col_kept // self.cols
        row_bits = [("row", 1 << bit) for bit in range(self.rows.bit_length() - 1)]
        col_bits = [("col", 1 << bit) for bit in range(self.cols.bit_length() - 1)]
        last = row_bits[-1:]
        early = col_bits + row_bits[:-1]
        turn = len(early) - 1 if early else 0
        first = early
        second = early[1:] + early[:1]
        third = early[turn:] + early[:turn]
        self.main = (first + last, second + last)
        self.rest = (third + last, third + last)

    def pairs(self, bits):
        found = []
        for row in range(self.rows):
            for col in range(self.cols):
                for seq in range(self.seqs):
                    axis, mask = bits[seq % 2]
                    other_row = row ^ mask if axis == "row" else row
                    other_col = col ^ mask if axis == "col" else col
                    found.append(
                        (
                            (row * self.cols + col) * self.seqs + seq,
                            (other_row * self.cols + other_col) * self.seqs + seq,
                        )
                    )
        return found

    def place(self, order, row, col):
        spot = 0
        for axis, mask in order:
            spot = spot * 2 + int(bool((row if axis == "row" else col) & mask))
        return spot

    def first_product(self):
        if self.split == 1:
            return 0, self.main
        return self.rows * self.per_row // 2 * BR, self.main[1:] + self.main[:1]

    def halve(self, part, orders, step):
        half = part.shape[0] // 2
        bits = (orders[0][step], orders[1][step])
        return part[:half] + lax.ppermute(part[half:], ("row", "col", "seq"), self.pairs(bits))


def body(plan, out_grads, layer_inputs, row_bits, col_bits, row_blocks, col_blocks):
    tokens, row_local = out_grads.shape[1:]
    col_local = layer_inputs.shape[2]
    tile = min(TILE, tokens)
    here = jnp.stack([lax.axis_index(name) for name in ("row", "col", "seq")]).astype(jnp.int32)
    scale = 1.0 / math.sqrt(row_local * plan.rows * col_local * plan.cols)
    left_rows = plan.rows * plan.per_row * BR
    right_cols = plan.cols * plan.per_col * BC
    inner = plan.per_row // plan.split
    cut = BR * 3 // 4
    cols_each = plan.per_col * BC
    blocks = plan.rows * plan.cols
    smem = pl.BlockSpec(memory_space=pltpu.SMEM)
    vmem = pl.BlockSpec(memory_space=pltpu.VMEM)
    main_shape = jax.ShapeDtypeStruct((blocks, inner * cut, cols_each), jnp.float32)
    rest_shape = jax.ShapeDtypeStruct((blocks, inner * (BR - cut), cols_each), jnp.float32)
    first_out, *factors = pl.pallas_call(
        functools.partial(mix_kernel, plan, scale),
        grid=(tokens // tile,),
        in_specs=[
            smem,
            smem,
            smem,
            pl.BlockSpec((tile, row_local), lambda step: (step, 0)),
            pl.BlockSpec((tile, col_local), lambda step: (step, 0)),
            vmem,
            vmem,
            vmem,
        ],
        out_specs=[vmem] * 5,
        out_shape=[
            main_shape,
            pltpu.VMEM((left_rows, tokens), jnp.bfloat16),
            pltpu.VMEM((left_rows, tokens), jnp.bfloat16),
            pltpu.VMEM((tokens, right_cols), jnp.bfloat16),
            pltpu.VMEM((tokens, right_cols), jnp.bfloat16),
        ],
        scratch_shapes=[
            pltpu.VMEM((row_local // CHUNK, CHUNK, tile), jnp.float32),
            pltpu.VMEM((col_local // CHUNK, tile, CHUNK), jnp.float32),
        ],
        compiler_params=pltpu.CompilerParams(vmem_limit_bytes=MIX_VMEM),
        name="mix",
    )(
        here,
        row_blocks,
        col_blocks,
        out_grads[0],
        layer_inputs[0],
        row_bits[None],
        col_bits[None],
        hadamard_table(CHUNK),
    )

    def products(wanted, shapes, name):
        return pl.pallas_call(
            functools.partial(product_kernel, plan, wanted),
            in_specs=[smem] + [vmem] * 4,
            out_specs=[vmem] * len(shapes),
            out_shape=shapes,
            compiler_params=pltpu.CompilerParams(vmem_limit_bytes=PRODUCT_VMEM),
            name=name,
        )(here, *factors)

    swap = [(0, 1), (1, 0)]
    half_rows = plan.rows * inner * BR
    main_rows = plan.rows * inner * cut
    if plan.split == 2:
        arrived = lax.ppermute(first_out, "seq", swap)
        (mine,) = products([(0, plan.main)], [main_shape], "main_product")
        rest_mine, rest_other = products(
            [(main_rows, plan.rest), (half_rows + main_rows, plan.rest)], [rest_shape] * 2, "rest_products"
        )
        main = mine + arrived
        rest = rest_mine + lax.ppermute(rest_other, "seq", swap)
    else:
        main = first_out
        (rest,) = products([(main_rows, plan.rest)], [rest_shape], "rest_product")
    steps = len(plan.main[0])
    for step in range(steps - 1):
        main = plan.halve(main, plan.main, step)
        rest = plan.halve(rest, plan.rest, step)
    both = plan.halve(jnp.concatenate([main, rest], axis=1), plan.rest, steps - 1)[0]

    def in_rows(values):
        first = values[..., : inner * cut, :].reshape(*values.shape[:-2], inner, cut, cols_each)
        second = values[..., inner * cut :, :].reshape(*values.shape[:-2], inner, BR - cut, cols_each)
        return jnp.concatenate([first, second], axis=-2)

    if plan.split == 2:
        both = in_rows(lax.all_gather(both, "seq", axis=0))
        return both.transpose(1, 0, 2, 3).reshape(1, plan.per_row * BR, cols_each)
    return in_rows(lax.psum(both, "seq")).reshape(1, plan.per_row * BR, cols_each)


def solution(mesh):
    def run(out_grads, layer_inputs, row_bits, col_bits, row_blocks, col_blocks):
        plan = Plan(mesh, row_blocks.shape[0], col_blocks.shape[0])
        in_specs = (P(None, "seq", "row"), P(None, "seq", "col"), P("row"), P("col"), P(), P())
        return jax.shard_map(
            lambda *args: body(plan, *args),
            mesh=mesh,
            in_specs=in_specs,
            out_specs=P(None, "row", "col"),
            check_vma=False,
        )(out_grads, layer_inputs, row_bits, col_bits, row_blocks, col_blocks)

    return run
```

```python
import functools
import math

import jax
import jax.numpy as jnp
from jax import lax
from jax.experimental import pallas as pl
from jax.experimental.pallas import tpu as pltpu
from jax.sharding import PartitionSpec as P

FF = 28672
BR = 64
BC = 128
CHUNK = 256
TILE = 256
MIX_VMEM = 30 << 20
PRODUCT_VMEM = 16 << 20


def scalar_parity(first, second):
    joined = first & second
    for shift in (8, 4, 2, 1):
        joined = joined ^ (joined >> shift)
    return joined & 1


def hadamard_table(order):
    first = lax.broadcasted_iota(jnp.int32, (order, order), 0)
    second = lax.broadcasted_iota(jnp.int32, (order, order), 1)
    return (1 - 2 * scalar_parity(first, second)).astype(jnp.float32).astype(jnp.bfloat16)


def mix_group(parts):
    first, second = parts[0] + parts[1], parts[0] - parts[1]
    third, fourth = parts[2] + parts[3], parts[2] - parts[3]
    return first + third, second + fourth, first - third, second - fourth


def kept_sum(source, slot, sign, width, length, axis):
    per_chunk = CHUNK // width
    inside = slot % per_chunk
    chunk = slot // per_chunk
    low, high = chunk % 4, chunk // 4
    start = pl.multiple_of(inside * width, width)
    total = None
    for group in range(source.shape[0] // 4):
        weight = sign * (1 - 2 * scalar_parity(high, jnp.int32(group))).astype(jnp.float32)
        if axis == 0:
            piece = source[4 * group + low, pl.ds(start, width), :]
        else:
            piece = source[4 * group + low, :, pl.ds(start, width)]
        total = piece * weight if total is None else total + piece * weight
    return total


def store_pieces(values, high_ref, low_ref, where):
    high = values.astype(jnp.bfloat16)
    high_ref[where] = high
    low_ref[where] = (values - high.astype(jnp.float32)).astype(jnp.bfloat16)


def product_blocks(plan, here, left_high, left_low, right_high, right_low, out_ref, first_row, orders):
    rows, width = out_ref.shape[1], out_ref.shape[2]
    tile = min(CHUNK, width)
    span = pl.ds(first_row, plan.rows * rows)
    seq = here[2] % 2
    for start in range(0, plan.cols * width, tile):
        lanes = pl.ds(start, tile)
        total = jnp.dot(left_high[span, :], right_high[:, lanes], preferred_element_type=jnp.float32)
        total += jnp.dot(left_high[span, :], right_low[:, lanes], preferred_element_type=jnp.float32)
        total += jnp.dot(left_low[span, :], right_high[:, lanes], preferred_element_type=jnp.float32)
        col = start // width
        for row in range(plan.rows):
            places = [plan.place(order, row, col) for order in orders]
            place = jnp.where(seq == 0, places[0], places[1]) if places[0] != places[1] else places[0]
            out_ref[place, :, pl.ds(start % width, tile)] = total[row * rows : (row + 1) * rows, :]


def mix_kernel(
    plan, scale, here, row_blocks, col_blocks, grads, inputs, row_bits, col_bits,
    out, left_high, left_low, right_high, right_low, row_mixed, col_mixed,
):
    step = pl.program_id(0)
    tokens, row_local = grads.shape
    col_local = inputs.shape[1]
    mixing = hadamard_table(CHUNK)
    index = lax.broadcasted_iota(jnp.int32, (1, row_local), 1) + here[0] * row_local
    row_sign = jnp.where(index < FF, 1 - 2 * row_bits[...], 0).astype(jnp.float32).astype(jnp.bfloat16)
    col_sign = (1 - 2 * col_bits[...]).astype(jnp.float32).astype(jnp.bfloat16)

    for group in range(row_local // CHUNK // 4):
        parts = []
        for chunk in range(4 * group, 4 * group + 4):
            lanes = slice(chunk * CHUNK, (chunk + 1) * CHUNK)
            signed = grads[:, lanes] * row_sign[:, lanes]
            parts.append(
                lax.dot_general(mixing, signed, (((1,), (1,)), ((), ())), preferred_element_type=jnp.float32)
            )
        for at, part in enumerate(mix_group(parts)):
            row_mixed[4 * group + at] = part
    for group in range(col_local // CHUNK // 4):
        parts = []
        for chunk in range(4 * group, 4 * group + 4):
            lanes = slice(chunk * CHUNK, (chunk + 1) * CHUNK)
            signed = inputs[:, lanes] * col_sign[:, lanes]
            parts.append(jnp.dot(signed, mixing, preferred_element_type=jnp.float32))
        for at, part in enumerate(mix_group(parts)):
            col_mixed[4 * group + at] = part

    now = pl.ds(pl.multiple_of(step * tokens, tokens), tokens)
    row_slots = row_local // BR
    inner = plan.per_row // plan.split
    cut = BR * 3 // 4
    for part in range(plan.split):
        base = part * plan.rows * inner * BR
        for row in range(plan.rows):
            for at in range(inner):
                kept = (here[0] ^ row) * plan.per_row + at * plan.split
                if plan.split == 2:
                    kept = kept + (here[2] ^ part)
                block = row_blocks[kept]
                sign = (1 - 2 * scalar_parity(block // row_slots, here[0])).astype(jnp.float32) * scale
                values = kept_sum(row_mixed, block % row_slots, sign, BR, tokens, 0)
                spot = row * inner + at
                first = base + spot * cut
                store_pieces(values[:cut], left_high, left_low, (pl.ds(first, cut), now))
                first = base + plan.rows * inner * cut + spot * (BR - cut)
                store_pieces(values[cut:], left_high, left_low, (pl.ds(first, BR - cut), now))
    col_slots = col_local // BC
    for col in range(plan.cols):
        for at in range(plan.per_col):
            block = col_blocks[(here[1] ^ col) * plan.per_col + at]
            sign = (1 - 2 * scalar_parity(block // col_slots, here[1])).astype(jnp.float32)
            values = kept_sum(col_mixed, block % col_slots, sign, BC, tokens, 1)
            store_pieces(values, right_high, right_low, (now, pl.ds((col * plan.per_col + at) * BC, BC)))

    @pl.when(step == pl.num_programs(0) - 1)
    def _():
        first, orders = plan.first_product()
        product_blocks(plan, here, left_high, left_low, right_high, right_low, out, first, orders)


def product_kernel(plan, wanted, here, left_high, left_low, right_high, right_low, *outs):
    for (first, orders), out in zip(wanted, outs):
        product_blocks(plan, here, left_high, left_low, right_high, right_low, out, first, orders)


class Plan:
    def __init__(self, mesh, row_kept, col_kept):
        self.rows, self.cols, self.seqs = mesh.shape["row"], mesh.shape["col"], mesh.shape["seq"]
        self.split = self.seqs if self.seqs == 2 and (row_kept // self.rows) % 2 == 0 else 1
        self.per_row = row_kept // self.rows
        self.per_col = col_kept // self.cols
        row_bits = [("row", 1 << bit) for bit in range(self.rows.bit_length() - 1)]
        col_bits = [("col", 1 << bit) for bit in range(self.cols.bit_length() - 1)]
        last = row_bits[-1:]
        early = col_bits + row_bits[:-1]
        turn = len(early) - 1 if early else 0
        first = early
        second = early[1:] + early[:1]
        third = early[turn:] + early[:turn]
        self.main = (first + last, second + last)
        self.rest = (third + last, third + last)

    def pairs(self, bits):
        found = []
        for row in range(self.rows):
            for col in range(self.cols):
                for seq in range(self.seqs):
                    axis, mask = bits[seq % 2]
                    other_row = row ^ mask if axis == "row" else row
                    other_col = col ^ mask if axis == "col" else col
                    found.append(
                        (
                            (row * self.cols + col) * self.seqs + seq,
                            (other_row * self.cols + other_col) * self.seqs + seq,
                        )
                    )
        return found

    def place(self, order, row, col):
        spot = 0
        for axis, mask in order:
            spot = spot * 2 + int(bool((row if axis == "row" else col) & mask))
        return spot

    def first_product(self):
        if self.split == 1:
            return 0, self.main
        return self.rows * self.per_row // 2 * BR, self.main[1:] + self.main[:1]

    def halve(self, part, orders, step):
        half = part.shape[0] // 2
        bits = (orders[0][step], orders[1][step])
        return part[:half] + lax.ppermute(part[half:], ("row", "col", "seq"), self.pairs(bits))


def body(plan, out_grads, layer_inputs, row_bits, col_bits, row_blocks, col_blocks):
    tokens, row_local = out_grads.shape[1:]
    col_local = layer_inputs.shape[2]
    tile = min(TILE, tokens)
    here = jnp.stack([lax.axis_index(name) for name in ("row", "col", "seq")]).astype(jnp.int32)
    scale = 1.0 / math.sqrt(row_local * plan.rows * col_local * plan.cols)
    left_rows = plan.rows * plan.per_row * BR
    right_cols = plan.cols * plan.per_col * BC
    inner = plan.per_row // plan.split
    cut = BR * 3 // 4
    cols_each = plan.per_col * BC
    blocks = plan.rows * plan.cols
    smem = pl.BlockSpec(memory_space=pltpu.SMEM)
    vmem = pl.BlockSpec(memory_space=pltpu.VMEM)
    main_shape = jax.ShapeDtypeStruct((blocks, inner * cut, cols_each), jnp.float32)
    rest_shape = jax.ShapeDtypeStruct((blocks, inner * (BR - cut), cols_each), jnp.float32)
    first_out, *factors = pl.pallas_call(
        functools.partial(mix_kernel, plan, scale),
        grid=(tokens // tile,),
        in_specs=[
            smem,
            smem,
            smem,
            pl.BlockSpec((tile, row_local), lambda step: (step, 0)),
            pl.BlockSpec((tile, col_local), lambda step: (step, 0)),
            pl.BlockSpec((1, row_local), lambda step: (0, 0)),
            pl.BlockSpec((1, col_local), lambda step: (0, 0)),
        ],
        out_specs=[vmem] * 5,
        out_shape=[
            main_shape,
            pltpu.VMEM((left_rows, tokens), jnp.bfloat16),
            pltpu.VMEM((left_rows, tokens), jnp.bfloat16),
            pltpu.VMEM((tokens, right_cols), jnp.bfloat16),
            pltpu.VMEM((tokens, right_cols), jnp.bfloat16),
        ],
        scratch_shapes=[
            pltpu.VMEM((row_local // CHUNK, CHUNK, tile), jnp.float32),
            pltpu.VMEM((col_local // CHUNK, tile, CHUNK), jnp.float32),
        ],
        compiler_params=pltpu.CompilerParams(vmem_limit_bytes=MIX_VMEM),
        name="mix",
    )(
        here,
        row_blocks,
        col_blocks,
        *(pltpu.with_memory_space_constraint(array, pltpu.HBM) for array in (out_grads[0], layer_inputs[0])),
        *(pltpu.with_memory_space_constraint(bits[None], pltpu.HBM) for bits in (row_bits, col_bits)),
    )

    def products(wanted, shapes, name):
        return pl.pallas_call(
            functools.partial(product_kernel, plan, wanted),
            in_specs=[smem] + [vmem] * 4,
            out_specs=[vmem] * len(shapes),
            out_shape=shapes,
            compiler_params=pltpu.CompilerParams(vmem_limit_bytes=PRODUCT_VMEM),
            name=name,
        )(here, *factors)

    swap = [(0, 1), (1, 0)]
    half_rows = plan.rows * inner * BR
    main_rows = plan.rows * inner * cut
    if plan.split == 2:
        arrived = lax.ppermute(first_out, "seq", swap)
        (mine,) = products([(0, plan.main)], [main_shape], "main_product")
        rest_mine, rest_other = products(
            [(main_rows, plan.rest), (half_rows + main_rows, plan.rest)], [rest_shape] * 2, "rest_products"
        )
        main = mine + arrived
        rest = rest_mine + lax.ppermute(rest_other, "seq", swap)
    else:
        main = first_out
        (rest,) = products([(main_rows, plan.rest)], [rest_shape], "rest_product")
    steps = len(plan.main[0])
    for step in range(steps - 1):
        main = plan.halve(main, plan.main, step)
        rest = plan.halve(rest, plan.rest, step)
    both = plan.halve(jnp.concatenate([main, rest], axis=1), plan.rest, steps - 1)[0]

    def in_rows(values):
        first = values[..., : inner * cut, :].reshape(*values.shape[:-2], inner, cut, cols_each)
        second = values[..., inner * cut :, :].reshape(*values.shape[:-2], inner, BR - cut, cols_each)
        return jnp.concatenate([first, second], axis=-2)

    if plan.split == 2:
        both = in_rows(lax.all_gather(both, "seq", axis=0))
        return both.transpose(1, 0, 2, 3).reshape(1, plan.per_row * BR, cols_each)
    return in_rows(lax.psum(both, "seq")).reshape(1, plan.per_row * BR, cols_each)


def solution(mesh):
    def run(out_grads, layer_inputs, row_bits, col_bits, row_blocks, col_blocks):
        plan = Plan(mesh, row_blocks.shape[0], col_blocks.shape[0])
        in_specs = (P(None, "seq", "row"), P(None, "seq", "col"), P("row"), P("col"), P(), P())
        return jax.shard_map(
            lambda *args: body(plan, *args),
            mesh=mesh,
            in_specs=in_specs,
            out_specs=P(None, "row", "col"),
            check_vma=False,
        )(out_grads, layer_inputs, row_bits, col_bits, row_blocks, col_blocks)

    return run
```

```python
import functools
import math

import jax
import jax.numpy as jnp
from jax import lax
from jax.experimental import pallas as pl
from jax.experimental.pallas import tpu as pltpu
from jax.sharding import PartitionSpec as P

FF = 28672
BR = 64
BC = 128
CHUNK = 256
TILE = 256
MIX_VMEM = 30 << 20
PRODUCT_VMEM = 16 << 20


def scalar_parity(first, second):
    joined = first & second
    for shift in (8, 4, 2, 1):
        joined = joined ^ (joined >> shift)
    return joined & 1


def hadamard_table(order):
    first = lax.broadcasted_iota(jnp.int32, (order, order), 0)
    second = lax.broadcasted_iota(jnp.int32, (order, order), 1)
    return (1 - 2 * scalar_parity(first, second)).astype(jnp.float32).astype(jnp.bfloat16)


def mix_group(parts):
    first, second = parts[0] + parts[1], parts[0] - parts[1]
    third, fourth = parts[2] + parts[3], parts[2] - parts[3]
    return first + third, second + fourth, first - third, second - fourth


def kept_sum(source, slot, sign, width, length, axis):
    per_chunk = CHUNK // width
    inside = slot % per_chunk
    chunk = slot // per_chunk
    low, high = chunk % 4, chunk // 4
    start = pl.multiple_of(inside * width, width)
    total = None
    for group in range(source.shape[0] // 4):
        weight = sign * (1 - 2 * scalar_parity(high, jnp.int32(group))).astype(jnp.float32)
        if axis == 0:
            piece = source[4 * group + low, pl.ds(start, width), :]
        else:
            piece = source[4 * group + low, :, pl.ds(start, width)]
        total = piece * weight if total is None else total + piece * weight
    return total


def store_pieces(values, high_ref, low_ref, where):
    high = values.astype(jnp.bfloat16)
    high_ref[where] = high
    low_ref[where] = (values - high.astype(jnp.float32)).astype(jnp.bfloat16)


def product_blocks(plan, here, factors, out_ref, first_row, orders, begin):
    left_high, left_low, right_high, right_low = factors
    count, rows, width = out_ref.shape
    tile = min(CHUNK, width)

    def run(order):
        for start in range(0, plan.cols * width, tile):
            col = start // width
            places = [plan.place(order, row, col) - begin for row in plan.row_sequence]
            wanted = [spot for spot, place in enumerate(places) if 0 <= place < count]
            while wanted:
                length = 1
                while length < len(wanted) and wanted[length] == wanted[0] + length:
                    length += 1
                span = pl.ds(first_row + wanted[0] * rows, length * rows)
                lanes = pl.ds(start, tile)
                total = jnp.dot(left_high[span, :], right_high[:, lanes], preferred_element_type=jnp.float32)
                total += jnp.dot(left_high[span, :], right_low[:, lanes], preferred_element_type=jnp.float32)
                total += jnp.dot(left_low[span, :], right_high[:, lanes], preferred_element_type=jnp.float32)
                for at in range(length):
                    piece = total[at * rows : (at + 1) * rows, :]
                    out_ref[places[wanted[at]], :, pl.ds(start % width, tile)] = piece
                wanted = wanted[length:]

    if orders[0] == orders[1]:
        run(orders[0])
    else:
        for seq, order in enumerate(orders):
            pl.when(here[2] % 2 == seq)(functools.partial(run, order))


def mix_kernel(
    plan, scale, here, row_blocks, col_blocks, grads, inputs, row_bits, col_bits,
    out, left_high, left_low, right_high, right_low, row_mixed, col_mixed,
):
    step = pl.program_id(0)
    tokens, row_local = grads.shape
    col_local = inputs.shape[1]
    mixing = hadamard_table(CHUNK)
    index = lax.broadcasted_iota(jnp.int32, (1, row_local), 1) + here[0] * row_local
    row_sign = jnp.where(index < FF, 1 - 2 * row_bits[...], 0).astype(jnp.float32).astype(jnp.bfloat16)
    col_sign = (1 - 2 * col_bits[...]).astype(jnp.float32).astype(jnp.bfloat16)

    for group in range(row_local // CHUNK // 4):
        parts = []
        for chunk in range(4 * group, 4 * group + 4):
            lanes = slice(chunk * CHUNK, (chunk + 1) * CHUNK)
            signed = grads[:, lanes] * row_sign[:, lanes]
            parts.append(
                lax.dot_general(mixing, signed, (((1,), (1,)), ((), ())), preferred_element_type=jnp.float32)
            )
        for at, part in enumerate(mix_group(parts)):
            row_mixed[4 * group + at] = part
    for group in range(col_local // CHUNK // 4):
        parts = []
        for chunk in range(4 * group, 4 * group + 4):
            lanes = slice(chunk * CHUNK, (chunk + 1) * CHUNK)
            signed = inputs[:, lanes] * col_sign[:, lanes]
            parts.append(jnp.dot(signed, mixing, preferred_element_type=jnp.float32))
        for at, part in enumerate(mix_group(parts)):
            col_mixed[4 * group + at] = part

    now = pl.ds(pl.multiple_of(step * tokens, tokens), tokens)
    row_slots = row_local // BR
    inner = plan.per_row // plan.split
    cut = BR * 3 // 4
    for part in range(plan.split):
        base = part * plan.rows * inner * BR
        for order, row in enumerate(plan.row_sequence):
            for at in range(inner):
                kept = (here[0] ^ row) * plan.per_row + at * plan.split
                if plan.split == 2:
                    kept = kept + (here[2] ^ part)
                block = row_blocks[kept]
                sign = (1 - 2 * scalar_parity(block // row_slots, here[0])).astype(jnp.float32) * scale
                values = kept_sum(row_mixed, block % row_slots, sign, BR, tokens, 0)
                spot = order * inner + at
                first = base + spot * cut
                store_pieces(values[:cut], left_high, left_low, (pl.ds(first, cut), now))
                first = base + plan.rows * inner * cut + spot * (BR - cut)
                store_pieces(values[cut:], left_high, left_low, (pl.ds(first, BR - cut), now))
    col_slots = col_local // BC
    for col in range(plan.cols):
        for at in range(plan.per_col):
            block = col_blocks[(here[1] ^ col) * plan.per_col + at]
            sign = (1 - 2 * scalar_parity(block // col_slots, here[1])).astype(jnp.float32)
            values = kept_sum(col_mixed, block % col_slots, sign, BC, tokens, 1)
            store_pieces(values, right_high, right_low, (now, pl.ds((col * plan.per_col + at) * BC, BC)))

    @pl.when(step == pl.num_programs(0) - 1)
    def _():
        factors = (left_high, left_low, right_high, right_low)
        product_blocks(plan, here, factors, out, *plan.first_product())


def product_kernel(plan, wanted, here, left_high, left_low, right_high, right_low, *outs):
    factors = (left_high, left_low, right_high, right_low)
    for args, out in zip(wanted, outs):
        product_blocks(plan, here, factors, out, *args)


class Plan:
    def __init__(self, mesh, row_kept, col_kept):
        self.rows, self.cols, self.seqs = mesh.shape["row"], mesh.shape["col"], mesh.shape["seq"]
        self.split = self.seqs if self.seqs == 2 and (row_kept // self.rows) % 2 == 0 else 1
        self.per_row = row_kept // self.rows
        self.per_col = col_kept // self.cols
        low_first = range(self.rows.bit_length() - 2, -1, -1)
        self.row_sequence = [
            sum(((spot >> (self.rows.bit_length() - 2 - bit)) & 1) << bit for bit in low_first) for spot in range(self.rows)
        ]
        row_bits = [("row", 1 << bit) for bit in range(self.rows.bit_length() - 1)]
        col_bits = [("col", 1 << bit) for bit in range(self.cols.bit_length() - 1)]
        last = row_bits[-1:]
        early = col_bits + row_bits[:-1]
        turn = len(early) - 1 if early else 0
        first = early
        second = early[1:] + early[:1]
        third = early[turn:] + early[:turn]
        self.main = (first + last, second + last)
        self.rest = (third + last, third + last)

    def pairs(self, bits):
        found = []
        for row in range(self.rows):
            for col in range(self.cols):
                for seq in range(self.seqs):
                    axis, mask = bits[seq % 2]
                    other_row = row ^ mask if axis == "row" else row
                    other_col = col ^ mask if axis == "col" else col
                    found.append(
                        (
                            (row * self.cols + col) * self.seqs + seq,
                            (other_row * self.cols + other_col) * self.seqs + seq,
                        )
                    )
        return found

    def place(self, order, row, col):
        spot = 0
        for axis, mask in order:
            spot = spot * 2 + int(bool((row if axis == "row" else col) & mask))
        return spot

    def first_product(self):
        half = self.rows * self.cols // 2
        if self.split == 1:
            return 0, self.main, half
        return self.rows * self.per_row // 2 * BR, self.main[1:] + self.main[:1], half

    def cross(self, part, orders, step):
        bits = (orders[0][step], orders[1][step])
        return lax.ppermute(part, ("row", "col", "seq"), self.pairs(bits))

    def halve(self, part, orders, step):
        half = part.shape[0] // 2
        return part[:half] + self.cross(part[half:], orders, step)


def body(plan, out_grads, layer_inputs, row_bits, col_bits, row_blocks, col_blocks):
    tokens, row_local = out_grads.shape[1:]
    col_local = layer_inputs.shape[2]
    tile = min(TILE, tokens)
    here = jnp.stack([lax.axis_index(name) for name in ("row", "col", "seq")]).astype(jnp.int32)
    scale = 1.0 / math.sqrt(row_local * plan.rows * col_local * plan.cols)
    left_rows = plan.rows * plan.per_row * BR
    right_cols = plan.cols * plan.per_col * BC
    inner = plan.per_row // plan.split
    cut = BR * 3 // 4
    cols_each = plan.per_col * BC
    blocks = plan.rows * plan.cols
    smem = pl.BlockSpec(memory_space=pltpu.SMEM)
    vmem = pl.BlockSpec(memory_space=pltpu.VMEM)
    main_shape = jax.ShapeDtypeStruct((blocks // 2, inner * cut, cols_each), jnp.float32)
    rest_shape = jax.ShapeDtypeStruct((blocks, inner * (BR - cut), cols_each), jnp.float32)
    first_out, *factors = pl.pallas_call(
        functools.partial(mix_kernel, plan, scale),
        grid=(tokens // tile,),
        in_specs=[
            smem,
            smem,
            smem,
            pl.BlockSpec((tile, row_local), lambda step: (step, 0)),
            pl.BlockSpec((tile, col_local), lambda step: (step, 0)),
            pl.BlockSpec((1, row_local), lambda step: (0, 0)),
            pl.BlockSpec((1, col_local), lambda step: (0, 0)),
        ],
        out_specs=[vmem] * 5,
        out_shape=[
            main_shape,
            pltpu.VMEM((left_rows, tokens), jnp.bfloat16),
            pltpu.VMEM((left_rows, tokens), jnp.bfloat16),
            pltpu.VMEM((tokens, right_cols), jnp.bfloat16),
            pltpu.VMEM((tokens, right_cols), jnp.bfloat16),
        ],
        scratch_shapes=[
            pltpu.VMEM((row_local // CHUNK, CHUNK, tile), jnp.float32),
            pltpu.VMEM((col_local // CHUNK, tile, CHUNK), jnp.float32),
        ],
        compiler_params=pltpu.CompilerParams(vmem_limit_bytes=MIX_VMEM),
        name="mix",
    )(
        here,
        row_blocks,
        col_blocks,
        *(pltpu.with_memory_space_constraint(array, pltpu.HBM) for array in (out_grads[0], layer_inputs[0])),
        *(pltpu.with_memory_space_constraint(bits[None], pltpu.HBM) for bits in (row_bits, col_bits)),
    )

    def products(wanted, shapes, name):
        return pl.pallas_call(
            functools.partial(product_kernel, plan, wanted),
            in_specs=[smem] + [vmem] * 4,
            out_specs=[vmem] * len(shapes),
            out_shape=shapes,
            compiler_params=pltpu.CompilerParams(vmem_limit_bytes=PRODUCT_VMEM),
            name=name,
        )(here, *factors)

    half = blocks // 2
    half_rows = plan.rows * inner * BR
    main_rows = plan.rows * inner * cut

    def swap(values):
        return lax.ppermute(values, "seq", [(0, 1), (1, 0)])

    if plan.split == 2:
        (sent,) = products([(0, plan.main, half)], [main_shape], "sent_product")
        sent = sent + swap(first_out)
        rest, rest_other = products(
            [(main_rows, plan.rest, 0), (half_rows + main_rows, plan.rest, 0)], [rest_shape] * 2, "rest_products"
        )
        rest = rest + swap(rest_other)
        (kept_other,) = products([(half_rows, plan.main[1:] + plan.main[:1], 0)], [main_shape], "kept_other_product")
        (kept,) = products([(0, plan.main, 0)], [main_shape], "kept_product")
        kept = kept + swap(kept_other)
    else:
        sent = first_out
        (rest,) = products([(main_rows, plan.rest, 0)], [rest_shape], "rest_product")
        (kept,) = products([(0, plan.main, 0)], [main_shape], "kept_product")
    steps = len(plan.main[0])
    main = kept + plan.cross(sent, plan.main, 0)
    rest = plan.halve(rest, plan.rest, 0)
    for step in range(1, steps - 1):
        main = plan.halve(main, plan.main, step)
        rest = plan.halve(rest, plan.rest, step)
    both = plan.halve(jnp.concatenate([main, rest], axis=1), plan.rest, steps - 1)[0]

    def in_rows(values):
        first = values[: inner * cut].reshape(inner, cut, cols_each)
        second = values[inner * cut :].reshape(inner, BR - cut, cols_each)
        return jnp.concatenate([first, second], axis=1)

    if plan.split == 2:
        mine, other = in_rows(both), in_rows(swap(both))
        first = lax.axis_index("seq") == 0
        pair = jnp.stack([jnp.where(first, mine, other), jnp.where(first, other, mine)], axis=1)
        return pair.reshape(1, plan.per_row * BR, cols_each)
    return in_rows(lax.psum(both, "seq")).reshape(1, plan.per_row * BR, cols_each)


def solution(mesh):
    def run(out_grads, layer_inputs, row_bits, col_bits, row_blocks, col_blocks):
        plan = Plan(mesh, row_blocks.shape[0], col_blocks.shape[0])
        in_specs = (P(None, "seq", "row"), P(None, "seq", "col"), P("row"), P("col"), P(), P())
        return jax.shard_map(
            lambda *args: body(plan, *args),
            mesh=mesh,
            in_specs=in_specs,
            out_specs=P(None, "row", "col"),
            check_vma=False,
        )(out_grads, layer_inputs, row_bits, col_bits, row_blocks, col_blocks)

    return run
```

```python
import functools
import math

import jax
import jax.numpy as jnp
from jax import lax
from jax.experimental import pallas as pl
from jax.experimental.pallas import tpu as pltpu
from jax.sharding import PartitionSpec as P

FF = 28672
BR = 64
BC = 128
CHUNK = 256
TILE = 256
MIX_VMEM = 30 << 20
PRODUCT_VMEM = 16 << 20


def scalar_parity(first, second):
    joined = first & second
    for shift in (8, 4, 2, 1):
        joined = joined ^ (joined >> shift)
    return joined & 1


def hadamard_table(order):
    first = lax.broadcasted_iota(jnp.int32, (order, order), 0)
    second = lax.broadcasted_iota(jnp.int32, (order, order), 1)
    return (1 - 2 * scalar_parity(first, second)).astype(jnp.float32).astype(jnp.bfloat16)


def mix_group(parts):
    first, second = parts[0] + parts[1], parts[0] - parts[1]
    third, fourth = parts[2] + parts[3], parts[2] - parts[3]
    return first + third, second + fourth, first - third, second - fourth


def kept_sum(source, slot, sign, width, length, axis):
    per_chunk = CHUNK // width
    inside = slot % per_chunk
    chunk = slot // per_chunk
    low, high = chunk % 4, chunk // 4
    start = pl.multiple_of(inside * width, width)
    total = None
    for group in range(source.shape[0] // 4):
        weight = sign * (1 - 2 * scalar_parity(high, jnp.int32(group))).astype(jnp.float32)
        if axis == 0:
            piece = source[4 * group + low, pl.ds(start, width), :]
        else:
            piece = source[4 * group + low, :, pl.ds(start, width)]
        total = piece * weight if total is None else total + piece * weight
    return total


def store_pieces(values, high_ref, low_ref, where):
    high = values.astype(jnp.bfloat16)
    high_ref[where] = high
    low_ref[where] = (values - high.astype(jnp.float32)).astype(jnp.bfloat16)


def product_blocks(plan, here, factors, out_ref, first_row, orders, begin):
    left_high, left_low, right_high, right_low = factors
    count, rows, width = out_ref.shape
    tile = min(CHUNK, width)

    def run(order):
        for start in range(0, plan.cols * width, tile):
            col = start // width
            places = [plan.place(order, row, col) - begin for row in plan.row_sequence]
            wanted = [spot for spot, place in enumerate(places) if 0 <= place < count]
            while wanted:
                length = 1
                while length < len(wanted) and wanted[length] == wanted[0] + length:
                    length += 1
                span = pl.ds(first_row + wanted[0] * rows, length * rows)
                lanes = pl.ds(start, tile)
                total = jnp.dot(left_high[span, :], right_high[:, lanes], preferred_element_type=jnp.float32)
                total += jnp.dot(left_high[span, :], right_low[:, lanes], preferred_element_type=jnp.float32)
                total += jnp.dot(left_low[span, :], right_high[:, lanes], preferred_element_type=jnp.float32)
                for at in range(length):
                    piece = total[at * rows : (at + 1) * rows, :]
                    out_ref[places[wanted[at]], :, pl.ds(start % width, tile)] = piece
                wanted = wanted[length:]

    if orders[0] == orders[1]:
        run(orders[0])
    else:
        for seq, order in enumerate(orders):
            pl.when(here[2] % 2 == seq)(functools.partial(run, order))


def mix_kernel(
    plan, scale, here, row_blocks, col_blocks, grads, inputs, row_bits, col_bits,
    sent_out, kept_out, left_high, left_low, right_high, right_low, row_mixed, col_mixed,
):
    step = pl.program_id(0)
    tokens, row_local = grads.shape
    col_local = inputs.shape[1]
    mixing = hadamard_table(CHUNK)
    index = lax.broadcasted_iota(jnp.int32, (1, row_local), 1) + here[0] * row_local
    row_sign = jnp.where(index < FF, 1 - 2 * row_bits[...], 0).astype(jnp.float32).astype(jnp.bfloat16)
    col_sign = (1 - 2 * col_bits[...]).astype(jnp.float32).astype(jnp.bfloat16)

    for group in range(row_local // CHUNK // 4):
        parts = []
        for chunk in range(4 * group, 4 * group + 4):
            lanes = slice(chunk * CHUNK, (chunk + 1) * CHUNK)
            signed = grads[:, lanes] * row_sign[:, lanes]
            parts.append(
                lax.dot_general(mixing, signed, (((1,), (1,)), ((), ())), preferred_element_type=jnp.float32)
            )
        for at, part in enumerate(mix_group(parts)):
            row_mixed[4 * group + at] = part
    for group in range(col_local // CHUNK // 4):
        parts = []
        for chunk in range(4 * group, 4 * group + 4):
            lanes = slice(chunk * CHUNK, (chunk + 1) * CHUNK)
            signed = inputs[:, lanes] * col_sign[:, lanes]
            parts.append(jnp.dot(signed, mixing, preferred_element_type=jnp.float32))
        for at, part in enumerate(mix_group(parts)):
            col_mixed[4 * group + at] = part

    now = pl.ds(pl.multiple_of(step * tokens, tokens), tokens)
    row_slots = row_local // BR
    inner = plan.per_row // plan.split
    cut = BR * 3 // 4
    for part in range(plan.split):
        base = part * plan.rows * inner * BR
        for order, row in enumerate(plan.row_sequence):
            for at in range(inner):
                kept = (here[0] ^ row) * plan.per_row + at * plan.split
                if plan.split == 2:
                    kept = kept + (here[2] ^ part)
                block = row_blocks[kept]
                sign = (1 - 2 * scalar_parity(block // row_slots, here[0])).astype(jnp.float32) * scale
                values = kept_sum(row_mixed, block % row_slots, sign, BR, tokens, 0)
                spot = order * inner + at
                first = base + spot * cut
                store_pieces(values[:cut], left_high, left_low, (pl.ds(first, cut), now))
                first = base + plan.rows * inner * cut + spot * (BR - cut)
                store_pieces(values[cut:], left_high, left_low, (pl.ds(first, BR - cut), now))
    col_slots = col_local // BC
    for col in range(plan.cols):
        for at in range(plan.per_col):
            block = col_blocks[(here[1] ^ col) * plan.per_col + at]
            sign = (1 - 2 * scalar_parity(block // col_slots, here[1])).astype(jnp.float32)
            values = kept_sum(col_mixed, block % col_slots, sign, BC, tokens, 1)
            store_pieces(values, right_high, right_low, (now, pl.ds((col * plan.per_col + at) * BC, BC)))

    @pl.when(step == pl.num_programs(0) - 1)
    def _():
        factors = (left_high, left_low, right_high, right_low)
        first_row, orders = plan.first_product()
        product_blocks(plan, here, factors, sent_out, first_row, orders, sent_out.shape[0])
        product_blocks(plan, here, factors, kept_out, first_row, orders, 0)


def product_kernel(plan, wanted, here, left_high, left_low, right_high, right_low, *outs):
    factors = (left_high, left_low, right_high, right_low)
    for args, out in zip(wanted, outs):
        product_blocks(plan, here, factors, out, *args)


class Plan:
    def __init__(self, mesh, row_kept, col_kept):
        self.rows, self.cols, self.seqs = mesh.shape["row"], mesh.shape["col"], mesh.shape["seq"]
        self.split = self.seqs if self.seqs == 2 and (row_kept // self.rows) % 2 == 0 else 1
        self.per_row = row_kept // self.rows
        self.per_col = col_kept // self.cols
        low_first = range(self.rows.bit_length() - 2, -1, -1)
        self.row_sequence = [
            sum(((spot >> (self.rows.bit_length() - 2 - bit)) & 1) << bit for bit in low_first) for spot in range(self.rows)
        ]
        row_bits = [("row", 1 << bit) for bit in range(self.rows.bit_length() - 1)]
        col_bits = [("col", 1 << bit) for bit in range(self.cols.bit_length() - 1)]
        last = row_bits[-1:]
        early = col_bits + row_bits[:-1]
        turn = len(early) - 1 if early else 0
        first = early
        second = early[1:] + early[:1]
        third = early[turn:] + early[:turn]
        self.main = (first + last, second + last)
        self.rest = (third + last, third + last)

    def pairs(self, bits):
        found = []
        for row in range(self.rows):
            for col in range(self.cols):
                for seq in range(self.seqs):
                    axis, mask = bits[seq % 2]
                    other_row = row ^ mask if axis == "row" else row
                    other_col = col ^ mask if axis == "col" else col
                    found.append(
                        (
                            (row * self.cols + col) * self.seqs + seq,
                            (other_row * self.cols + other_col) * self.seqs + seq,
                        )
                    )
        return found

    def place(self, order, row, col):
        spot = 0
        for axis, mask in order:
            spot = spot * 2 + int(bool((row if axis == "row" else col) & mask))
        return spot

    def first_product(self):
        if self.split == 1:
            return 0, self.main
        return self.rows * self.per_row // 2 * BR, self.main[1:] + self.main[:1]

    def cross(self, part, orders, step):
        bits = (orders[0][step], orders[1][step])
        return lax.ppermute(part, ("row", "col", "seq"), self.pairs(bits))

    def halve(self, part, orders, step):
        half = part.shape[0] // 2
        return part[:half] + self.cross(part[half:], orders, step)


def body(plan, out_grads, layer_inputs, row_bits, col_bits, row_blocks, col_blocks):
    tokens, row_local = out_grads.shape[1:]
    col_local = layer_inputs.shape[2]
    tile = min(TILE, tokens)
    here = jnp.stack([lax.axis_index(name) for name in ("row", "col", "seq")]).astype(jnp.int32)
    scale = 1.0 / math.sqrt(row_local * plan.rows * col_local * plan.cols)
    left_rows = plan.rows * plan.per_row * BR
    right_cols = plan.cols * plan.per_col * BC
    inner = plan.per_row // plan.split
    cut = BR * 3 // 4
    cols_each = plan.per_col * BC
    blocks = plan.rows * plan.cols
    smem = pl.BlockSpec(memory_space=pltpu.SMEM)
    vmem = pl.BlockSpec(memory_space=pltpu.VMEM)
    main_shape = jax.ShapeDtypeStruct((blocks // 2, inner * cut, cols_each), jnp.float32)
    rest_shape = jax.ShapeDtypeStruct((blocks, inner * (BR - cut), cols_each), jnp.float32)
    first_sent, first_kept, *factors = pl.pallas_call(
        functools.partial(mix_kernel, plan, scale),
        grid=(tokens // tile,),
        in_specs=[
            smem,
            smem,
            smem,
            pl.BlockSpec((tile, row_local), lambda step: (step, 0)),
            pl.BlockSpec((tile, col_local), lambda step: (step, 0)),
            pl.BlockSpec((1, row_local), lambda step: (0, 0)),
            pl.BlockSpec((1, col_local), lambda step: (0, 0)),
        ],
        out_specs=[vmem] * 6,
        out_shape=[
            main_shape,
            main_shape,
            pltpu.VMEM((left_rows, tokens), jnp.bfloat16),
            pltpu.VMEM((left_rows, tokens), jnp.bfloat16),
            pltpu.VMEM((tokens, right_cols), jnp.bfloat16),
            pltpu.VMEM((tokens, right_cols), jnp.bfloat16),
        ],
        scratch_shapes=[
            pltpu.VMEM((row_local // CHUNK, CHUNK, tile), jnp.float32),
            pltpu.VMEM((col_local // CHUNK, tile, CHUNK), jnp.float32),
        ],
        compiler_params=pltpu.CompilerParams(vmem_limit_bytes=MIX_VMEM),
        name="mix",
    )(
        here,
        pltpu.with_memory_space_constraint(row_blocks, pltpu.HBM),
        pltpu.with_memory_space_constraint(col_blocks, pltpu.HBM),
        *(pltpu.with_memory_space_constraint(array, pltpu.HBM) for array in (out_grads[0], layer_inputs[0])),
        *(pltpu.with_memory_space_constraint(bits[None], pltpu.HBM) for bits in (row_bits, col_bits)),
    )

    def products(wanted, shapes, name, here=here):
        return pl.pallas_call(
            functools.partial(product_kernel, plan, wanted),
            in_specs=[smem] + [vmem] * 4,
            out_specs=[vmem] * len(shapes),
            out_shape=shapes,
            compiler_params=pltpu.CompilerParams(vmem_limit_bytes=PRODUCT_VMEM),
            name=name,
        )(here, *factors)

    half = blocks // 2
    half_rows = plan.rows * inner * BR
    main_rows = plan.rows * inner * cut

    def swap(values):
        return lax.ppermute(values, "seq", [(0, 1), (1, 0)])

    if plan.split == 2:
        arrived_sent, arrived_kept = swap(first_sent), swap(first_kept)
        (sent,) = products([(0, plan.main, half)], [main_shape], "sent_product")
        sent = sent + arrived_sent
        later, sent = lax.optimization_barrier((here, sent))
        rest, rest_other = products(
            [(main_rows, plan.rest, 0), (half_rows + main_rows, plan.rest, 0)], [rest_shape] * 2, "rest_products", later
        )
        rest = rest + swap(rest_other)
        (kept,) = products([(0, plan.main, 0)], [main_shape], "kept_product", later)
        kept = kept + arrived_kept
    else:
        sent, kept = first_sent, first_kept
        (rest,) = products([(main_rows, plan.rest, 0)], [rest_shape], "rest_product")
    steps = len(plan.main[0])
    main = kept + plan.cross(sent, plan.main, 0)
    rest = plan.halve(rest, plan.rest, 0)
    for step in range(1, steps - 1):
        main = plan.halve(main, plan.main, step)
        arrived = plan.cross(rest[rest.shape[0] // 2 :], plan.rest, step)
        main, arrived = lax.optimization_barrier((main, arrived))
        rest = rest[: rest.shape[0] // 2] + arrived
    both = plan.halve(jnp.concatenate([main, rest], axis=1), plan.rest, steps - 1)[0]

    def in_rows(values):
        first = values[: inner * cut].reshape(inner, cut, cols_each)
        second = values[inner * cut :].reshape(inner, BR - cut, cols_each)
        return jnp.concatenate([first, second], axis=1)

    if plan.split == 2:
        mine, other = in_rows(both), in_rows(swap(both))
        first = lax.axis_index("seq") == 0
        pair = jnp.stack([jnp.where(first, mine, other), jnp.where(first, other, mine)], axis=1)
        return pair.reshape(1, plan.per_row * BR, cols_each)
    return in_rows(lax.psum(both, "seq")).reshape(1, plan.per_row * BR, cols_each)


def solution(mesh):
    def run(out_grads, layer_inputs, row_bits, col_bits, row_blocks, col_blocks):
        plan = Plan(mesh, row_blocks.shape[0], col_blocks.shape[0])
        in_specs = (P(None, "seq", "row"), P(None, "seq", "col"), P("row"), P("col"), P(), P())
        return jax.shard_map(
            lambda *args: body(plan, *args),
            mesh=mesh,
            in_specs=in_specs,
            out_specs=P(None, "row", "col"),
            check_vma=False,
        )(out_grads, layer_inputs, row_bits, col_bits, row_blocks, col_blocks)

    return run
```

```python
import functools
import math

import jax
import jax.numpy as jnp
from jax import lax
from jax.experimental import pallas as pl
from jax.experimental.pallas import tpu as pltpu
from jax.sharding import PartitionSpec as P

FF = 28672
BR = 64
BC = 128
CHUNK = 256
TILE = 256
MIX_VMEM = 30 << 20
PRODUCT_VMEM = 16 << 20


def scalar_parity(first, second):
    joined = first & second
    for shift in (8, 4, 2, 1):
        joined = joined ^ (joined >> shift)
    return joined & 1


def hadamard_table(order):
    first = lax.broadcasted_iota(jnp.int32, (order, order), 0)
    second = lax.broadcasted_iota(jnp.int32, (order, order), 1)
    return (1 - 2 * scalar_parity(first, second)).astype(jnp.float32).astype(jnp.bfloat16)


def mix_group(parts):
    first, second = parts[0] + parts[1], parts[0] - parts[1]
    third, fourth = parts[2] + parts[3], parts[2] - parts[3]
    return first + third, second + fourth, first - third, second - fourth


def kept_sum(source, slot, sign, width, length, axis):
    per_chunk = CHUNK // width
    inside = slot % per_chunk
    chunk = slot // per_chunk
    low, high = chunk % 4, chunk // 4
    start = pl.multiple_of(inside * width, width)
    total = None
    for group in range(source.shape[0] // 4):
        weight = sign * (1 - 2 * scalar_parity(high, jnp.int32(group))).astype(jnp.float32)
        if axis == 0:
            piece = source[4 * group + low, pl.ds(start, width), :]
        else:
            piece = source[4 * group + low, :, pl.ds(start, width)]
        total = piece * weight if total is None else total + piece * weight
    return total


def store_pieces(values, high_ref, low_ref, where):
    high = values.astype(jnp.bfloat16)
    high_ref[where] = high
    low_ref[where] = (values - high.astype(jnp.float32)).astype(jnp.bfloat16)


def product_blocks(plan, here, factors, out_ref, first_row, orders, begin):
    left_high, left_low, right_high, right_low = factors
    count, rows, width = out_ref.shape
    tile = min(CHUNK, width)

    def run(order):
        for start in range(0, plan.cols * width, tile):
            col = start // width
            places = [plan.place(order, row, col) - begin for row in plan.row_sequence]
            wanted = [spot for spot, place in enumerate(places) if 0 <= place < count]
            while wanted:
                length = 1
                while length < len(wanted) and wanted[length] == wanted[0] + length:
                    length += 1
                span = pl.ds(first_row + wanted[0] * rows, length * rows)
                lanes = pl.ds(start, tile)
                total = jnp.dot(left_high[span, :], right_high[:, lanes], preferred_element_type=jnp.float32)
                total += jnp.dot(left_high[span, :], right_low[:, lanes], preferred_element_type=jnp.float32)
                total += jnp.dot(left_low[span, :], right_high[:, lanes], preferred_element_type=jnp.float32)
                for at in range(length):
                    piece = total[at * rows : (at + 1) * rows, :]
                    out_ref[places[wanted[at]], :, pl.ds(start % width, tile)] = piece
                wanted = wanted[length:]

    if orders[0] == orders[1]:
        run(orders[0])
    else:
        for seq, order in enumerate(orders):
            pl.when(here[2] % 2 == seq)(functools.partial(run, order))


def mix_kernel(
    plan, scale, here, row_blocks, col_blocks, grads, inputs, row_bits, col_bits,
    sent_out, rest_out, left_high, left_low, right_high, right_low, row_mixed, col_mixed,
    signs, mixing_here,
):
    step = pl.program_id(0)
    tokens, row_local = grads.shape
    col_local = inputs.shape[1]

    @pl.when(step == 0)
    def _():
        mixing_here[...] = hadamard_table(CHUNK)
        index = lax.broadcasted_iota(jnp.int32, (1, row_local), 1) + here[0] * row_local
        signs[0:1, :row_local] = jnp.where(index < FF, 1 - 2 * row_bits[...], 0).astype(jnp.float32)
        signs[1:2, :col_local] = (1 - 2 * col_bits[...]).astype(jnp.float32)

    mixing = mixing_here[...]
    row_sign = signs[0:1, :row_local].astype(jnp.bfloat16)
    col_sign = signs[1:2, :col_local].astype(jnp.bfloat16)
    for group in range(row_local // CHUNK // 4):
        parts = []
        for chunk in range(4 * group, 4 * group + 4):
            lanes = slice(chunk * CHUNK, (chunk + 1) * CHUNK)
            signed = grads[:, lanes] * row_sign[:, lanes]
            parts.append(
                lax.dot_general(mixing, signed, (((1,), (1,)), ((), ())), preferred_element_type=jnp.float32)
            )
        for at, part in enumerate(mix_group(parts)):
            row_mixed[4 * group + at] = part
    for group in range(col_local // CHUNK // 4):
        parts = []
        for chunk in range(4 * group, 4 * group + 4):
            lanes = slice(chunk * CHUNK, (chunk + 1) * CHUNK)
            signed = inputs[:, lanes] * col_sign[:, lanes]
            parts.append(jnp.dot(signed, mixing, preferred_element_type=jnp.float32))
        for at, part in enumerate(mix_group(parts)):
            col_mixed[4 * group + at] = part

    now = pl.ds(pl.multiple_of(step * tokens, tokens), tokens)
    row_slots = row_local // BR
    inner = plan.per_row // plan.split
    cut = BR * 3 // 4
    for part in range(plan.split):
        base = part * plan.rows * inner * BR
        for order, row in enumerate(plan.row_sequence):
            for at in range(inner):
                kept = (here[0] ^ row) * plan.per_row + at * plan.split
                if plan.split == 2:
                    kept = kept + (here[2] ^ part)
                block = row_blocks[kept]
                sign = (1 - 2 * scalar_parity(block // row_slots, here[0])).astype(jnp.float32) * scale
                values = kept_sum(row_mixed, block % row_slots, sign, BR, tokens, 0)
                spot = order * inner + at
                first = base + spot * cut
                store_pieces(values[:cut], left_high, left_low, (pl.ds(first, cut), now))
                first = base + plan.rows * inner * cut + spot * (BR - cut)
                store_pieces(values[cut:], left_high, left_low, (pl.ds(first, BR - cut), now))
    col_slots = col_local // BC
    for col in range(plan.cols):
        for at in range(plan.per_col):
            block = col_blocks[(here[1] ^ col) * plan.per_col + at]
            sign = (1 - 2 * scalar_parity(block // col_slots, here[1])).astype(jnp.float32)
            values = kept_sum(col_mixed, block % col_slots, sign, BC, tokens, 1)
            store_pieces(values, right_high, right_low, (now, pl.ds((col * plan.per_col + at) * BC, BC)))

    @pl.when(step == pl.num_programs(0) - 1)
    def _():
        factors = (left_high, left_low, right_high, right_low)
        first_row, orders = plan.first_product()
        product_blocks(plan, here, factors, sent_out, first_row, orders, sent_out.shape[0])
        product_blocks(plan, here, factors, rest_out, first_row + plan.rows * inner * cut, plan.rest, 0)


def product_kernel(plan, wanted, here, left_high, left_low, right_high, right_low, *outs):
    factors = (left_high, left_low, right_high, right_low)
    for args, out in zip(wanted, outs):
        product_blocks(plan, here, factors, out, *args)


class Plan:
    def __init__(self, mesh, row_kept, col_kept):
        self.rows, self.cols, self.seqs = mesh.shape["row"], mesh.shape["col"], mesh.shape["seq"]
        self.split = self.seqs if self.seqs == 2 and (row_kept // self.rows) % 2 == 0 else 1
        self.per_row = row_kept // self.rows
        self.per_col = col_kept // self.cols
        low_first = range(self.rows.bit_length() - 2, -1, -1)
        self.row_sequence = [
            sum(((spot >> (self.rows.bit_length() - 2 - bit)) & 1) << bit for bit in low_first) for spot in range(self.rows)
        ]
        row_bits = [("row", 1 << bit) for bit in range(self.rows.bit_length() - 1)]
        col_bits = [("col", 1 << bit) for bit in range(self.cols.bit_length() - 1)]
        last = row_bits[-1:]
        early = col_bits + row_bits[:-1]
        turn = len(early) - 1 if early else 0
        first = early
        second = early[1:] + early[:1]
        third = early[turn:] + early[:turn]
        self.main = (first + last, second + last)
        self.rest = (third + last, third + last)

    def pairs(self, bits):
        found = []
        for row in range(self.rows):
            for col in range(self.cols):
                for seq in range(self.seqs):
                    axis, mask = bits[seq % 2]
                    other_row = row ^ mask if axis == "row" else row
                    other_col = col ^ mask if axis == "col" else col
                    found.append(
                        (
                            (row * self.cols + col) * self.seqs + seq,
                            (other_row * self.cols + other_col) * self.seqs + seq,
                        )
                    )
        return found

    def place(self, order, row, col):
        spot = 0
        for axis, mask in order:
            spot = spot * 2 + int(bool((row if axis == "row" else col) & mask))
        return spot

    def first_product(self):
        if self.split == 1:
            return 0, self.main
        return self.rows * self.per_row // 2 * BR, self.main[1:] + self.main[:1]

    def cross(self, part, orders, step):
        bits = (orders[0][step], orders[1][step])
        return lax.ppermute(part, ("row", "col", "seq"), self.pairs(bits))

    def halve(self, part, orders, step):
        half = part.shape[0] // 2
        return part[:half] + self.cross(part[half:], orders, step)


def body(plan, out_grads, layer_inputs, row_bits, col_bits, row_blocks, col_blocks):
    tokens, row_local = out_grads.shape[1:]
    col_local = layer_inputs.shape[2]
    tile = min(TILE, tokens)
    here = jnp.stack([lax.axis_index(name) for name in ("row", "col", "seq")]).astype(jnp.int32)
    scale = 1.0 / math.sqrt(row_local * plan.rows * col_local * plan.cols)
    left_rows = plan.rows * plan.per_row * BR
    right_cols = plan.cols * plan.per_col * BC
    inner = plan.per_row // plan.split
    cut = BR * 3 // 4
    cols_each = plan.per_col * BC
    blocks = plan.rows * plan.cols
    smem = pl.BlockSpec(memory_space=pltpu.SMEM)
    vmem = pl.BlockSpec(memory_space=pltpu.VMEM)
    main_shape = jax.ShapeDtypeStruct((blocks // 2, inner * cut, cols_each), jnp.float32)
    rest_shape = jax.ShapeDtypeStruct((blocks, inner * (BR - cut), cols_each), jnp.float32)
    first_sent, first_rest, *factors = pl.pallas_call(
        functools.partial(mix_kernel, plan, scale),
        grid=(tokens // tile,),
        in_specs=[
            smem,
            smem,
            smem,
            pl.BlockSpec((tile, row_local), lambda step: (step, 0)),
            pl.BlockSpec((tile, col_local), lambda step: (step, 0)),
            pl.BlockSpec((1, row_local), lambda step: (0, 0)),
            pl.BlockSpec((1, col_local), lambda step: (0, 0)),
        ],
        out_specs=[vmem] * 6,
        out_shape=[
            main_shape,
            rest_shape,
            pltpu.VMEM((left_rows, tokens), jnp.bfloat16),
            pltpu.VMEM((left_rows, tokens), jnp.bfloat16),
            pltpu.VMEM((tokens, right_cols), jnp.bfloat16),
            pltpu.VMEM((tokens, right_cols), jnp.bfloat16),
        ],
        scratch_shapes=[
            pltpu.VMEM((row_local // CHUNK, CHUNK, tile), jnp.float32),
            pltpu.VMEM((col_local // CHUNK, tile, CHUNK), jnp.float32),
            pltpu.VMEM((8, max(row_local, col_local)), jnp.float32),
            pltpu.VMEM((CHUNK, CHUNK), jnp.bfloat16),
        ],
        compiler_params=pltpu.CompilerParams(vmem_limit_bytes=MIX_VMEM),
        name="mix",
    )(
        here,
        pltpu.with_memory_space_constraint(row_blocks, pltpu.HBM),
        pltpu.with_memory_space_constraint(col_blocks, pltpu.HBM),
        *(pltpu.with_memory_space_constraint(array, pltpu.HBM) for array in (out_grads[0], layer_inputs[0])),
        *(pltpu.with_memory_space_constraint(bits[None], pltpu.HBM) for bits in (row_bits, col_bits)),
    )

    def products(wanted, shapes, name, here=here):
        return pl.pallas_call(
            functools.partial(product_kernel, plan, wanted),
            in_specs=[smem] + [vmem] * 4,
            out_specs=[vmem] * len(shapes),
            out_shape=shapes,
            compiler_params=pltpu.CompilerParams(vmem_limit_bytes=PRODUCT_VMEM),
            name=name,
        )(here, *factors)

    half = blocks // 2
    half_rows = plan.rows * inner * BR
    main_rows = plan.rows * inner * cut

    def swap(values):
        return lax.ppermute(values, "seq", [(0, 1), (1, 0)])

    if plan.split == 2:
        arrived_sent, arrived_rest = swap(first_sent), swap(first_rest)
        (sent,) = products([(0, plan.main, half)], [main_shape], "sent_product")
        sent = sent + arrived_sent
        later, sent = lax.optimization_barrier((here, sent))
        later, arrived_rest = lax.optimization_barrier((later, arrived_rest))
        (rest,) = products([(main_rows, plan.rest, 0)], [rest_shape], "rest_product", later)
        rest = rest + arrived_rest
        (kept_other,) = products([(half_rows, plan.main[1:] + plan.main[:1], 0)], [main_shape], "kept_other_product", later)
        (kept,) = products([(0, plan.main, 0)], [main_shape], "kept_product", later)
        main = lax.optimization_barrier(kept + plan.cross(sent, plan.main, 0)) + swap(kept_other)
    else:
        rest = first_rest
        (kept,) = products([(0, plan.main, 0)], [main_shape], "kept_product")
        main = kept + plan.cross(first_sent, plan.main, 0)
    steps = len(plan.main[0])
    rest = plan.halve(rest, plan.rest, 0)
    for step in range(1, steps - 1):
        main = plan.halve(main, plan.main, step)
        arrived = plan.cross(rest[rest.shape[0] // 2 :], plan.rest, step)
        main, arrived = lax.optimization_barrier((main, arrived))
        rest = rest[: rest.shape[0] // 2] + arrived
    both = plan.halve(jnp.concatenate([main, rest], axis=1), plan.rest, steps - 1)[0]

    def in_rows(values):
        first = values[: inner * cut].reshape(inner, cut, cols_each)
        second = values[inner * cut :].reshape(inner, BR - cut, cols_each)
        return jnp.concatenate([first, second], axis=1)

    if plan.split == 2:
        mine, other = in_rows(both), in_rows(swap(both))
        first = lax.axis_index("seq") == 0
        pair = jnp.stack([jnp.where(first, mine, other), jnp.where(first, other, mine)], axis=1)
        return pair.reshape(1, plan.per_row * BR, cols_each)
    return in_rows(lax.psum(both, "seq")).reshape(1, plan.per_row * BR, cols_each)


def solution(mesh):
    def run(out_grads, layer_inputs, row_bits, col_bits, row_blocks, col_blocks):
        plan = Plan(mesh, row_blocks.shape[0], col_blocks.shape[0])
        in_specs = (P(None, "seq", "row"), P(None, "seq", "col"), P("row"), P("col"), P(), P())
        return jax.shard_map(
            lambda *args: body(plan, *args),
            mesh=mesh,
            in_specs=in_specs,
            out_specs=P(None, "row", "col"),
            check_vma=False,
        )(out_grads, layer_inputs, row_bits, col_bits, row_blocks, col_blocks)

    return run
```

```python
import functools
import math

import jax
import jax.numpy as jnp
from jax import lax
from jax.experimental import pallas as pl
from jax.experimental.pallas import tpu as pltpu
from jax.sharding import PartitionSpec as P

FF = 28672
BR = 64
BC = 128
CHUNK = 256
TILE = 256
MIX_VMEM = 30 << 20
PRODUCT_VMEM = 16 << 20
AHEAD = 20 * 10**9


def scalar_parity(first, second):
    joined = first & second
    for shift in (8, 4, 2, 1):
        joined = joined ^ (joined >> shift)
    return joined & 1


def hadamard_table(order):
    first = lax.broadcasted_iota(jnp.int32, (order, order), 0)
    second = lax.broadcasted_iota(jnp.int32, (order, order), 1)
    return (1 - 2 * scalar_parity(first, second)).astype(jnp.float32).astype(jnp.bfloat16)


def mix_group(parts):
    first, second = parts[0] + parts[1], parts[0] - parts[1]
    third, fourth = parts[2] + parts[3], parts[2] - parts[3]
    return first + third, second + fourth, first - third, second - fourth


def kept_sum(source, slot, sign, width, length, axis):
    per_chunk = CHUNK // width
    inside = slot % per_chunk
    chunk = slot // per_chunk
    low, high = chunk % 4, chunk // 4
    start = pl.multiple_of(inside * width, width)
    total = None
    for group in range(source.shape[0] // 4):
        weight = sign * (1 - 2 * scalar_parity(high, jnp.int32(group))).astype(jnp.float32)
        if axis == 0:
            piece = source[4 * group + low, pl.ds(start, width), :]
        else:
            piece = source[4 * group + low, :, pl.ds(start, width)]
        total = piece * weight if total is None else total + piece * weight
    return total


def store_pieces(values, high_ref, low_ref, where):
    high = values.astype(jnp.bfloat16)
    high_ref[where] = high
    low_ref[where] = (values - high.astype(jnp.float32)).astype(jnp.bfloat16)


def product_blocks(plan, here, factors, out_ref, first_row, orders, begin):
    left_high, left_low, right_high, right_low = factors
    count, rows, width = out_ref.shape
    tile = min(CHUNK, width)

    def run(order):
        for start in range(0, plan.cols * width, tile):
            col = start // width
            places = [plan.place(order, row, col) - begin for row in plan.row_sequence]
            wanted = [spot for spot, place in enumerate(places) if 0 <= place < count]
            while wanted:
                length = 1
                while length < len(wanted) and wanted[length] == wanted[0] + length:
                    length += 1
                span = pl.ds(first_row + wanted[0] * rows, length * rows)
                lanes = pl.ds(start, tile)
                total = jnp.dot(left_high[span, :], right_high[:, lanes], preferred_element_type=jnp.float32)
                total += jnp.dot(left_high[span, :], right_low[:, lanes], preferred_element_type=jnp.float32)
                total += jnp.dot(left_low[span, :], right_high[:, lanes], preferred_element_type=jnp.float32)
                for at in range(length):
                    piece = total[at * rows : (at + 1) * rows, :]
                    out_ref[places[wanted[at]], :, pl.ds(start % width, tile)] = piece
                wanted = wanted[length:]

    if orders[0] == orders[1]:
        run(orders[0])
    else:
        for seq, order in enumerate(orders):
            pl.when(here[2] % 2 == seq)(functools.partial(run, order))


def device_place():
    return [lax.axis_index(name) for name in ("row", "col", "seq")]


def mix_kernel(
    plan, scale, row_blocks, col_blocks, grads, inputs, row_bits, col_bits,
    sent_out, left_high, left_low, right_high, right_low, row_mixed, col_mixed,
    signs, mixing_here,
):
    here = device_place()
    step = pl.program_id(0)
    tokens, row_local = grads.shape
    col_local = inputs.shape[1]

    @pl.when(step == 0)
    def _():
        mixing_here[...] = hadamard_table(CHUNK)
        index = lax.broadcasted_iota(jnp.int32, (1, row_local), 1) + here[0] * row_local
        signs[0:1, :row_local] = jnp.where(index < FF, 1 - 2 * row_bits[...], 0).astype(jnp.float32)
        signs[1:2, :col_local] = (1 - 2 * col_bits[...]).astype(jnp.float32)

    mixing = mixing_here[...]
    row_sign = signs[0:1, :row_local].astype(jnp.bfloat16)
    col_sign = signs[1:2, :col_local].astype(jnp.bfloat16)
    for group in range(row_local // CHUNK // 4):
        parts = []
        for chunk in range(4 * group, 4 * group + 4):
            lanes = slice(chunk * CHUNK, (chunk + 1) * CHUNK)
            signed = grads[:, lanes] * row_sign[:, lanes]
            parts.append(
                lax.dot_general(mixing, signed, (((1,), (1,)), ((), ())), preferred_element_type=jnp.float32)
            )
        for at, part in enumerate(mix_group(parts)):
            row_mixed[4 * group + at] = part
    for group in range(col_local // CHUNK // 4):
        parts = []
        for chunk in range(4 * group, 4 * group + 4):
            lanes = slice(chunk * CHUNK, (chunk + 1) * CHUNK)
            signed = inputs[:, lanes] * col_sign[:, lanes]
            parts.append(jnp.dot(signed, mixing, preferred_element_type=jnp.float32))
        for at, part in enumerate(mix_group(parts)):
            col_mixed[4 * group + at] = part

    now = pl.ds(pl.multiple_of(step * tokens, tokens), tokens)
    row_slots = row_local // BR
    inner = plan.per_row // plan.split
    cut = BR * 3 // 4
    for part in range(plan.split):
        base = part * plan.rows * inner * BR
        for order, row in enumerate(plan.row_sequence):
            for at in range(inner):
                kept = (here[0] ^ row) * plan.per_row + at * plan.split
                if plan.split == 2:
                    kept = kept + (here[2] ^ part)
                block = row_blocks[kept]
                sign = (1 - 2 * scalar_parity(block // row_slots, here[0])).astype(jnp.float32) * scale
                values = kept_sum(row_mixed, block % row_slots, sign, BR, tokens, 0)
                spot = order * inner + at
                first = base + spot * cut
                store_pieces(values[:cut], left_high, left_low, (pl.ds(first, cut), now))
                first = base + plan.rows * inner * cut + spot * (BR - cut)
                store_pieces(values[cut:], left_high, left_low, (pl.ds(first, BR - cut), now))
    col_slots = col_local // BC
    for col in range(plan.cols):
        for at in range(plan.per_col):
            block = col_blocks[(here[1] ^ col) * plan.per_col + at]
            sign = (1 - 2 * scalar_parity(block // col_slots, here[1])).astype(jnp.float32)
            values = kept_sum(col_mixed, block % col_slots, sign, BC, tokens, 1)
            store_pieces(values, right_high, right_low, (now, pl.ds((col * plan.per_col + at) * BC, BC)))

    @pl.when(step == pl.num_programs(0) - 1)
    def _():
        factors = (left_high, left_low, right_high, right_low)
        first_row, orders = plan.first_product()
        product_blocks(plan, here, factors, sent_out, first_row, orders, sent_out.shape[0])


def product_kernel(plan, wanted, after, left_high, left_low, right_high, right_low, *outs):
    here = device_place()
    factors = (left_high, left_low, right_high, right_low)
    for args, out in zip(wanted, outs):
        product_blocks(plan, here, factors, out, *args)


def add_kernel(first, second, out):
    out[...] = first[...] + second[...]


def add_early(first, second):
    vmem = pl.BlockSpec(memory_space=pltpu.VMEM)
    return pl.pallas_call(
        add_kernel,
        in_specs=[vmem] * 2,
        out_specs=vmem,
        out_shape=jax.ShapeDtypeStruct(first.shape, first.dtype),
        compiler_params=pltpu.CompilerParams(vmem_limit_bytes=PRODUCT_VMEM),
        cost_estimate=pl.CostEstimate(flops=AHEAD, bytes_accessed=AHEAD // 100, transcendentals=0),
        name="add_early",
    )(first, second)


class Plan:
    def __init__(self, mesh, row_kept, col_kept):
        self.rows, self.cols, self.seqs = mesh.shape["row"], mesh.shape["col"], mesh.shape["seq"]
        self.split = self.seqs if self.seqs == 2 and (row_kept // self.rows) % 2 == 0 else 1
        self.per_row = row_kept // self.rows
        self.per_col = col_kept // self.cols
        low_first = range(self.rows.bit_length() - 2, -1, -1)
        self.row_sequence = [
            sum(((spot >> (self.rows.bit_length() - 2 - bit)) & 1) << bit for bit in low_first) for spot in range(self.rows)
        ]
        row_bits = [("row", 1 << bit) for bit in range(self.rows.bit_length() - 1)]
        col_bits = [("col", 1 << bit) for bit in range(self.cols.bit_length() - 1)]
        last = row_bits[-1:]
        early = col_bits + row_bits[:-1]
        turn = len(early) - 1 if early else 0
        first = early
        second = early[1:] + early[:1]
        third = early[turn:] + early[:turn]
        self.main = (first + last, second + last)
        self.rest = (third + last, third + last)

    def pairs(self, bits):
        found = []
        for row in range(self.rows):
            for col in range(self.cols):
                for seq in range(self.seqs):
                    axis, mask = bits[seq % 2]
                    other_row = row ^ mask if axis == "row" else row
                    other_col = col ^ mask if axis == "col" else col
                    found.append(
                        (
                            (row * self.cols + col) * self.seqs + seq,
                            (other_row * self.cols + other_col) * self.seqs + seq,
                        )
                    )
        return found

    def place(self, order, row, col):
        spot = 0
        for axis, mask in order:
            spot = spot * 2 + int(bool((row if axis == "row" else col) & mask))
        return spot

    def first_product(self):
        if self.split == 1:
            return 0, self.main
        return self.rows * self.per_row // 2 * BR, self.main[1:] + self.main[:1]

    def cross(self, part, orders, step):
        bits = (orders[0][step], orders[1][step])
        return lax.ppermute(part, ("row", "col", "seq"), self.pairs(bits))

    def halve(self, part, orders, step):
        half = part.shape[0] // 2
        return part[:half] + self.cross(part[half:], orders, step)


def body(plan, out_grads, layer_inputs, row_bits, col_bits, row_blocks, col_blocks):
    tokens, row_local = out_grads.shape[1:]
    col_local = layer_inputs.shape[2]
    tile = min(TILE, tokens)
    start = jnp.zeros((8, 128), jnp.float32)
    scale = 1.0 / math.sqrt(row_local * plan.rows * col_local * plan.cols)
    left_rows = plan.rows * plan.per_row * BR
    right_cols = plan.cols * plan.per_col * BC
    inner = plan.per_row // plan.split
    cut = BR * 3 // 4
    cols_each = plan.per_col * BC
    blocks = plan.rows * plan.cols
    smem = pl.BlockSpec(memory_space=pltpu.SMEM)
    vmem = pl.BlockSpec(memory_space=pltpu.VMEM)
    main_shape = jax.ShapeDtypeStruct((blocks // 2, inner * cut, cols_each), jnp.float32)
    rest_shape = jax.ShapeDtypeStruct((blocks, inner * (BR - cut), cols_each), jnp.float32)
    first_sent, *factors = pl.pallas_call(
        functools.partial(mix_kernel, plan, scale),
        grid=(tokens // tile,),
        in_specs=[
            smem,
            smem,
            pl.BlockSpec((tile, row_local), lambda step: (step, 0)),
            pl.BlockSpec((tile, col_local), lambda step: (step, 0)),
            pl.BlockSpec((1, row_local), lambda step: (0, 0)),
            pl.BlockSpec((1, col_local), lambda step: (0, 0)),
        ],
        out_specs=[vmem] * 5,
        out_shape=[
            main_shape,
            pltpu.VMEM((left_rows, tokens), jnp.bfloat16),
            pltpu.VMEM((left_rows, tokens), jnp.bfloat16),
            pltpu.VMEM((tokens, right_cols), jnp.bfloat16),
            pltpu.VMEM((tokens, right_cols), jnp.bfloat16),
        ],
        scratch_shapes=[
            pltpu.VMEM((row_local // CHUNK, CHUNK, tile), jnp.float32),
            pltpu.VMEM((col_local // CHUNK, tile, CHUNK), jnp.float32),
            pltpu.VMEM((8, max(row_local, col_local)), jnp.float32),
            pltpu.VMEM((CHUNK, CHUNK), jnp.bfloat16),
        ],
        compiler_params=pltpu.CompilerParams(vmem_limit_bytes=MIX_VMEM),
        name="mix",
    )(
        pltpu.with_memory_space_constraint(row_blocks, pltpu.HBM),
        pltpu.with_memory_space_constraint(col_blocks, pltpu.HBM),
        *(pltpu.with_memory_space_constraint(array, pltpu.HBM) for array in (out_grads[0], layer_inputs[0])),
        *(pltpu.with_memory_space_constraint(bits[None], pltpu.HBM) for bits in (row_bits, col_bits)),
    )

    def products(wanted, shapes, name, after=start):
        return pl.pallas_call(
            functools.partial(product_kernel, plan, wanted),
            in_specs=[pl.BlockSpec(memory_space=pl.ANY)] + [vmem] * 4,
            out_specs=[vmem] * len(shapes),
            out_shape=shapes,
            compiler_params=pltpu.CompilerParams(vmem_limit_bytes=PRODUCT_VMEM),
            name=name,
        )(after, *factors)

    half = blocks // 2
    half_rows = plan.rows * inner * BR
    main_rows = plan.rows * inner * cut

    def swap(values):
        return lax.ppermute(values, "seq", [(0, 1), (1, 0)])

    if plan.split == 2:
        arrived_sent = swap(first_sent)
        sent, rest_other = products(
            [(0, plan.main, half), (half_rows + main_rows, plan.rest, 0)], [main_shape, rest_shape], "sent_products"
        )
        sent = sent + arrived_sent
        later, sent = lax.optimization_barrier((start, sent))
        after, arrived_rest = lax.optimization_barrier((later, swap(rest_other)))
        (rest,) = products([(main_rows, plan.rest, 0)], [rest_shape], "rest_product", after)
        rest = rest + arrived_rest
        (kept_other,) = products([(half_rows, plan.main[1:] + plan.main[:1], 0)], [main_shape], "kept_other_product", later)
        (kept,) = products([(0, plan.main, 0)], [main_shape], "kept_product", later)
        main = add_early(kept, plan.cross(sent, plan.main, 0)) + swap(kept_other)
    else:
        (rest,) = products([(main_rows, plan.rest, 0)], [rest_shape], "rest_product")
        (kept,) = products([(0, plan.main, 0)], [main_shape], "kept_product")
        main = kept + plan.cross(first_sent, plan.main, 0)
    steps = len(plan.main[0])
    rest = plan.halve(rest, plan.rest, 0)
    for step in range(1, steps - 1):
        main = plan.halve(main, plan.main, step)
        arrived = plan.cross(rest[rest.shape[0] // 2 :], plan.rest, step)
        main, arrived = lax.optimization_barrier((main, arrived))
        rest = rest[: rest.shape[0] // 2] + arrived
    both = plan.halve(jnp.concatenate([main, rest], axis=1), plan.rest, steps - 1)[0]

    def in_rows(values):
        first = values[: inner * cut].reshape(inner, cut, cols_each)
        second = values[inner * cut :].reshape(inner, BR - cut, cols_each)
        return jnp.concatenate([first, second], axis=1)

    if plan.split == 2:
        mine, other = in_rows(both), in_rows(swap(both))
        first = lax.axis_index("seq") == 0
        pair = jnp.stack([jnp.where(first, mine, other), jnp.where(first, other, mine)], axis=1)
        return pair.reshape(1, plan.per_row * BR, cols_each)
    return in_rows(lax.psum(both, "seq")).reshape(1, plan.per_row * BR, cols_each)


def solution(mesh):
    def run(out_grads, layer_inputs, row_bits, col_bits, row_blocks, col_blocks):
        plan = Plan(mesh, row_blocks.shape[0], col_blocks.shape[0])
        in_specs = (P(None, "seq", "row"), P(None, "seq", "col"), P("row"), P("col"), P(), P())
        return jax.shard_map(
            lambda *args: body(plan, *args),
            mesh=mesh,
            in_specs=in_specs,
            out_specs=P(None, "row", "col"),
            check_vma=False,
        )(out_grads, layer_inputs, row_bits, col_bits, row_blocks, col_blocks)

    return run
```

```python
import functools
import math

import jax
import jax.numpy as jnp
from jax import lax
from jax.experimental import pallas as pl
from jax.experimental.pallas import tpu as pltpu
from jax.sharding import PartitionSpec as P

FF = 28672
BR = 64
BC = 128
CHUNK = 256
TILE = 256
MIX_VMEM = 30 << 20
PRODUCT_VMEM = 16 << 20
AHEAD = 20 * 10**9


def scalar_parity(first, second):
    joined = first & second
    for shift in (8, 4, 2, 1):
        joined = joined ^ (joined >> shift)
    return joined & 1


def hadamard_table(order):
    first = lax.broadcasted_iota(jnp.int32, (order, order), 0)
    second = lax.broadcasted_iota(jnp.int32, (order, order), 1)
    return (1 - 2 * scalar_parity(first, second)).astype(jnp.float32).astype(jnp.bfloat16)


def mix_group(parts):
    first, second = parts[0] + parts[1], parts[0] - parts[1]
    third, fourth = parts[2] + parts[3], parts[2] - parts[3]
    return first + third, second + fourth, first - third, second - fourth


def kept_sum(source, slot, sign, width, length, axis):
    per_chunk = CHUNK // width
    inside = slot % per_chunk
    chunk = slot // per_chunk
    low, high = chunk % 4, chunk // 4
    start = pl.multiple_of(inside * width, width)
    total = None
    for group in range(source.shape[0] // 4):
        weight = sign * (1 - 2 * scalar_parity(high, jnp.int32(group))).astype(jnp.float32)
        if axis == 0:
            piece = source[4 * group + low, pl.ds(start, width), :]
        else:
            piece = source[4 * group + low, :, pl.ds(start, width)]
        total = piece * weight if total is None else total + piece * weight
    return total


def store_pieces(values, high_ref, low_ref, where):
    high = values.astype(jnp.bfloat16)
    high_ref[where] = high
    low_ref[where] = (values - high.astype(jnp.float32)).astype(jnp.bfloat16)


def product_blocks(plan, here, factors, wanted):
    left_high, left_low, right_high, right_low = factors
    width = wanted[0][0].shape[2]
    tile = min(CHUNK, width)

    def run(seq):
        for start in range(0, plan.cols * width, tile):
            pieces = []
            for out_ref, first_row, orders, begin in wanted:
                count, rows, _ = out_ref.shape
                for spot, row in enumerate(plan.row_sequence):
                    place = plan.place(orders[seq], row, start // width) - begin
                    if 0 <= place < count:
                        pieces.append((first_row + spot * rows, rows, place, out_ref))
            pieces.sort(key=lambda piece: piece[0])
            while pieces:
                length = 1
                while length < len(pieces) and pieces[length][0] == sum(pieces[length - 1][:2]):
                    length += 1
                base, end = pieces[0][0], sum(pieces[length - 1][:2])
                span, lanes = pl.ds(base, end - base), pl.ds(start, tile)
                total = jnp.dot(left_high[span, :], right_high[:, lanes], preferred_element_type=jnp.float32)
                total += jnp.dot(left_high[span, :], right_low[:, lanes], preferred_element_type=jnp.float32)
                total += jnp.dot(left_low[span, :], right_high[:, lanes], preferred_element_type=jnp.float32)
                for at, rows, place, out_ref in pieces[:length]:
                    out_ref[place, :, pl.ds(start % width, tile)] = total[at - base : at - base + rows, :]
                pieces = pieces[length:]

    if all(orders[0] == orders[1] for _, _, orders, _ in wanted):
        run(0)
    else:
        for seq in range(2):
            pl.when(here[2] % 2 == seq)(functools.partial(run, seq))


def device_place():
    return [lax.axis_index(name) for name in ("row", "col", "seq")]


def mix_kernel(
    plan, scale, row_blocks, col_blocks, grads, inputs, row_bits, col_bits,
    sent_out, left_high, left_low, right_high, right_low, row_mixed, col_mixed,
    signs, mixing_here,
):
    here = device_place()
    step = pl.program_id(0)
    tokens, row_local = grads.shape
    col_local = inputs.shape[1]

    @pl.when(step == 0)
    def _():
        mixing_here[...] = hadamard_table(CHUNK)
        index = lax.broadcasted_iota(jnp.int32, (1, row_local), 1) + here[0] * row_local
        signs[0:1, :row_local] = jnp.where(index < FF, 1 - 2 * row_bits[...], 0).astype(jnp.float32)
        signs[1:2, :col_local] = (1 - 2 * col_bits[...]).astype(jnp.float32)

    mixing = mixing_here[...]
    row_sign = signs[0:1, :row_local].astype(jnp.bfloat16)
    col_sign = signs[1:2, :col_local].astype(jnp.bfloat16)
    for group in range(row_local // CHUNK // 4):
        parts = []
        for chunk in range(4 * group, 4 * group + 4):
            lanes = slice(chunk * CHUNK, (chunk + 1) * CHUNK)
            signed = grads[:, lanes] * row_sign[:, lanes]
            parts.append(
                lax.dot_general(mixing, signed, (((1,), (1,)), ((), ())), preferred_element_type=jnp.float32)
            )
        for at, part in enumerate(mix_group(parts)):
            row_mixed[4 * group + at] = part
    for group in range(col_local // CHUNK // 4):
        parts = []
        for chunk in range(4 * group, 4 * group + 4):
            lanes = slice(chunk * CHUNK, (chunk + 1) * CHUNK)
            signed = inputs[:, lanes] * col_sign[:, lanes]
            parts.append(jnp.dot(signed, mixing, preferred_element_type=jnp.float32))
        for at, part in enumerate(mix_group(parts)):
            col_mixed[4 * group + at] = part

    now = pl.ds(pl.multiple_of(step * tokens, tokens), tokens)
    row_slots = row_local // BR
    inner = plan.per_row // plan.split
    cut = BR * 3 // 4
    for part in range(plan.split):
        for order, row in enumerate(plan.row_sequence):
            for at in range(inner):
                kept = (here[0] ^ row) * plan.per_row + at * plan.split
                if plan.split == 2:
                    kept = kept + (here[2] ^ part)
                block = row_blocks[kept]
                sign = (1 - 2 * scalar_parity(block // row_slots, here[0])).astype(jnp.float32) * scale
                values = kept_sum(row_mixed, block % row_slots, sign, BR, tokens, 0)
                spot = order * inner + at
                first = plan.first_row(part, 0) + spot * cut
                store_pieces(values[:cut], left_high, left_low, (pl.ds(first, cut), now))
                first = plan.first_row(part, 1) + spot * (BR - cut)
                store_pieces(values[cut:], left_high, left_low, (pl.ds(first, BR - cut), now))
    col_slots = col_local // BC
    for col in range(plan.cols):
        for at in range(plan.per_col):
            block = col_blocks[(here[1] ^ col) * plan.per_col + at]
            sign = (1 - 2 * scalar_parity(block // col_slots, here[1])).astype(jnp.float32)
            values = kept_sum(col_mixed, block % col_slots, sign, BC, tokens, 1)
            store_pieces(values, right_high, right_low, (now, pl.ds((col * plan.per_col + at) * BC, BC)))

    @pl.when(step == pl.num_programs(0) - 1)
    def _():
        factors = (left_high, left_low, right_high, right_low)
        orders = plan.main if plan.split == 1 else plan.main[1:] + plan.main[:1]
        first_row = plan.first_row(plan.split - 1, 0)
        product_blocks(plan, here, factors, [(sent_out, first_row, orders, sent_out.shape[0])])


def product_kernel(plan, wanted, after, left_high, left_low, right_high, right_low, *outs):
    here = device_place()
    factors = (left_high, left_low, right_high, right_low)
    product_blocks(plan, here, factors, [(out, *args) for args, out in zip(wanted, outs)])


def add_kernel(first, second, out):
    out[...] = first[...] + second[...]


def add_early(first, second):
    vmem = pl.BlockSpec(memory_space=pltpu.VMEM)
    return pl.pallas_call(
        add_kernel,
        in_specs=[vmem] * 2,
        out_specs=vmem,
        out_shape=jax.ShapeDtypeStruct(first.shape, first.dtype),
        compiler_params=pltpu.CompilerParams(vmem_limit_bytes=PRODUCT_VMEM),
        cost_estimate=pl.CostEstimate(flops=AHEAD, bytes_accessed=AHEAD // 100, transcendentals=0),
        name="add_early",
    )(first, second)


class Plan:
    def __init__(self, mesh, row_kept, col_kept):
        self.rows, self.cols, self.seqs = mesh.shape["row"], mesh.shape["col"], mesh.shape["seq"]
        self.split = self.seqs if self.seqs == 2 and (row_kept // self.rows) % 2 == 0 else 1
        self.per_row = row_kept // self.rows
        self.per_col = col_kept // self.cols
        low_first = range(self.rows.bit_length() - 2, -1, -1)
        self.row_sequence = [
            sum(((spot >> (self.rows.bit_length() - 2 - bit)) & 1) << bit for bit in low_first) for spot in range(self.rows)
        ]
        row_bits = [("row", 1 << bit) for bit in range(self.rows.bit_length() - 1)]
        col_bits = [("col", 1 << bit) for bit in range(self.cols.bit_length() - 1)]
        last = row_bits[-1:]
        early = col_bits + row_bits[:-1]
        turn = len(early) - 1 if early else 0
        first = early
        second = early[1:] + early[:1]
        third = early[turn:] + early[:turn]
        self.main = (first + last, second + last)
        self.rest = (third + last, third + last)

    def pairs(self, bits):
        found = []
        for row in range(self.rows):
            for col in range(self.cols):
                for seq in range(self.seqs):
                    axis, mask = bits[seq % 2]
                    other_row = row ^ mask if axis == "row" else row
                    other_col = col ^ mask if axis == "col" else col
                    found.append(
                        (
                            (row * self.cols + col) * self.seqs + seq,
                            (other_row * self.cols + other_col) * self.seqs + seq,
                        )
                    )
        return found

    def place(self, order, row, col):
        spot = 0
        for axis, mask in order:
            spot = spot * 2 + int(bool((row if axis == "row" else col) & mask))
        return spot

    def first_row(self, part, kind):
        inner = self.per_row // self.split * self.rows
        main, rest = inner * (BR * 3 // 4), inner * (BR - BR * 3 // 4)
        if self.split == 1:
            return (0, main)[kind]
        return ((0, main + rest), (main + 2 * rest, main))[part][kind]

    def cross(self, part, orders, step):
        bits = (orders[0][step], orders[1][step])
        return lax.ppermute(part, ("row", "col", "seq"), self.pairs(bits))

    def halve(self, part, orders, step):
        half = part.shape[0] // 2
        return part[:half] + self.cross(part[half:], orders, step)


def body(plan, out_grads, layer_inputs, row_bits, col_bits, row_blocks, col_blocks):
    tokens, row_local = out_grads.shape[1:]
    col_local = layer_inputs.shape[2]
    tile = min(TILE, tokens)
    start = jnp.zeros((8, 128), jnp.float32)
    scale = 1.0 / math.sqrt(row_local * plan.rows * col_local * plan.cols)
    left_rows = plan.rows * plan.per_row * BR
    right_cols = plan.cols * plan.per_col * BC
    inner = plan.per_row // plan.split
    cut = BR * 3 // 4
    cols_each = plan.per_col * BC
    blocks = plan.rows * plan.cols
    smem = pl.BlockSpec(memory_space=pltpu.SMEM)
    vmem = pl.BlockSpec(memory_space=pltpu.VMEM)
    main_shape = jax.ShapeDtypeStruct((blocks // 2, inner * cut, cols_each), jnp.float32)
    rest_shape = jax.ShapeDtypeStruct((blocks, inner * (BR - cut), cols_each), jnp.float32)
    first_sent, *factors = pl.pallas_call(
        functools.partial(mix_kernel, plan, scale),
        grid=(tokens // tile,),
        in_specs=[
            smem,
            smem,
            pl.BlockSpec((tile, row_local), lambda step: (step, 0)),
            pl.BlockSpec((tile, col_local), lambda step: (step, 0)),
            pl.BlockSpec((1, row_local), lambda step: (0, 0)),
            pl.BlockSpec((1, col_local), lambda step: (0, 0)),
        ],
        out_specs=[vmem] * 5,
        out_shape=[
            main_shape,
            pltpu.VMEM((left_rows, tokens), jnp.bfloat16),
            pltpu.VMEM((left_rows, tokens), jnp.bfloat16),
            pltpu.VMEM((tokens, right_cols), jnp.bfloat16),
            pltpu.VMEM((tokens, right_cols), jnp.bfloat16),
        ],
        scratch_shapes=[
            pltpu.VMEM((row_local // CHUNK, CHUNK, tile), jnp.float32),
            pltpu.VMEM((col_local // CHUNK, tile, CHUNK), jnp.float32),
            pltpu.VMEM((8, max(row_local, col_local)), jnp.float32),
            pltpu.VMEM((CHUNK, CHUNK), jnp.bfloat16),
        ],
        compiler_params=pltpu.CompilerParams(vmem_limit_bytes=MIX_VMEM),
        name="mix",
    )(
        pltpu.with_memory_space_constraint(row_blocks, pltpu.HBM),
        pltpu.with_memory_space_constraint(col_blocks, pltpu.HBM),
        *(pltpu.with_memory_space_constraint(array, pltpu.HBM) for array in (out_grads[0], layer_inputs[0])),
        *(pltpu.with_memory_space_constraint(bits[None], pltpu.HBM) for bits in (row_bits, col_bits)),
    )

    def products(wanted, shapes, name, after=start):
        return pl.pallas_call(
            functools.partial(product_kernel, plan, wanted),
            in_specs=[pl.BlockSpec(memory_space=pl.ANY)] + [vmem] * 4,
            out_specs=[vmem] * len(shapes),
            out_shape=shapes,
            compiler_params=pltpu.CompilerParams(vmem_limit_bytes=PRODUCT_VMEM),
            name=name,
        )(after, *factors)

    half = blocks // 2

    def swap(values):
        return lax.ppermute(values, "seq", [(0, 1), (1, 0)])

    if plan.split == 2:
        arrived_sent = swap(first_sent)
        sent, rest_other = products(
            [(0, plan.main, half), (plan.first_row(1, 1), plan.rest, 0)], [main_shape, rest_shape], "sent_products"
        )
        sent = sent + arrived_sent
        later, sent = lax.optimization_barrier((start, sent))
        after, arrived_rest = lax.optimization_barrier((later, swap(rest_other)))
        (rest,) = products([(plan.first_row(0, 1), plan.rest, 0)], [rest_shape], "rest_product", after)
        rest = rest + arrived_rest
        (kept_other,) = products([(plan.first_row(1, 0), plan.main[1:] + plan.main[:1], 0)], [main_shape], "kept_other_product", later)
        (kept,) = products([(0, plan.main, 0)], [main_shape], "kept_product", later)
        main = add_early(kept, plan.cross(sent, plan.main, 0)) + swap(kept_other)
    else:
        (rest,) = products([(plan.first_row(0, 1), plan.rest, 0)], [rest_shape], "rest_product")
        (kept,) = products([(0, plan.main, 0)], [main_shape], "kept_product")
        main = kept + plan.cross(first_sent, plan.main, 0)
    steps = len(plan.main[0])
    rest = plan.halve(rest, plan.rest, 0)
    for step in range(1, steps - 1):
        main = plan.halve(main, plan.main, step)
        arrived = plan.cross(rest[rest.shape[0] // 2 :], plan.rest, step)
        main, arrived = lax.optimization_barrier((main, arrived))
        rest = rest[: rest.shape[0] // 2] + arrived
    both = plan.halve(jnp.concatenate([main, rest], axis=1), plan.rest, steps - 1)[0]

    def in_rows(values):
        first = values[: inner * cut].reshape(inner, cut, cols_each)
        second = values[inner * cut :].reshape(inner, BR - cut, cols_each)
        return jnp.concatenate([first, second], axis=1)

    if plan.split == 2:
        mine, other = in_rows(both), in_rows(swap(both))
        first = lax.axis_index("seq") == 0
        pair = jnp.stack([jnp.where(first, mine, other), jnp.where(first, other, mine)], axis=1)
        return pair.reshape(1, plan.per_row * BR, cols_each)
    return in_rows(lax.psum(both, "seq")).reshape(1, plan.per_row * BR, cols_each)


def solution(mesh):
    def run(out_grads, layer_inputs, row_bits, col_bits, row_blocks, col_blocks):
        plan = Plan(mesh, row_blocks.shape[0], col_blocks.shape[0])
        in_specs = (P(None, "seq", "row"), P(None, "seq", "col"), P("row"), P("col"), P(), P())
        return jax.shard_map(
            lambda *args: body(plan, *args),
            mesh=mesh,
            in_specs=in_specs,
            out_specs=P(None, "row", "col"),
            check_vma=False,
        )(out_grads, layer_inputs, row_bits, col_bits, row_blocks, col_blocks)

    return run
```

```python
import functools
import math

import jax
import jax.numpy as jnp
from jax import lax
from jax.experimental import pallas as pl
from jax.experimental.pallas import tpu as pltpu
from jax.sharding import PartitionSpec as P

FF = 28672
BR = 64
BC = 128
CHUNK = 256
TILE = 256
MIX_VMEM = 30 << 20
PRODUCT_VMEM = 16 << 20
PRODUCT_TILE = 512
AHEAD = 20 * 10**9


def scalar_parity(first, second):
    joined = first & second
    for shift in (8, 4, 2, 1):
        joined = joined ^ (joined >> shift)
    return joined & 1


def hadamard_table(order):
    first = lax.broadcasted_iota(jnp.int32, (order, order), 0)
    second = lax.broadcasted_iota(jnp.int32, (order, order), 1)
    return (1 - 2 * scalar_parity(first, second)).astype(jnp.float32).astype(jnp.bfloat16)


def mix_group(parts):
    first, second = parts[0] + parts[1], parts[0] - parts[1]
    third, fourth = parts[2] + parts[3], parts[2] - parts[3]
    return first + third, second + fourth, first - third, second - fourth


def kept_sum(source, slot, sign, width, length, axis):
    per_chunk = CHUNK // width
    inside = slot % per_chunk
    chunk = slot // per_chunk
    low, high = chunk % 4, chunk // 4
    start = pl.multiple_of(inside * width, width)
    total = None
    for group in range(source.shape[0] // 4):
        weight = sign * (1 - 2 * scalar_parity(high, jnp.int32(group))).astype(jnp.float32)
        if axis == 0:
            piece = source[4 * group + low, pl.ds(start, width), :]
        else:
            piece = source[4 * group + low, :, pl.ds(start, width)]
        total = piece * weight if total is None else total + piece * weight
    return total


def store_pieces(values, high_ref, low_ref, where):
    high = values.astype(jnp.bfloat16)
    high_ref[where] = high
    low_ref[where] = (values - high.astype(jnp.float32)).astype(jnp.bfloat16)


def product_blocks(plan, here, factors, wanted):
    left_high, left_low, right_high, right_low = factors
    width = wanted[0][0].shape[2]
    tile = min(PRODUCT_TILE, width)

    def run(seq):
        for start in range(0, plan.cols * width, tile):
            pieces = []
            for out_ref, first_row, orders, begin in wanted:
                count, rows, _ = out_ref.shape
                for spot, row in enumerate(plan.row_sequence):
                    place = plan.place(orders[seq], row, start // width) - begin
                    if 0 <= place < count:
                        pieces.append((first_row + spot * rows, rows, place, out_ref))
            pieces.sort(key=lambda piece: piece[0])
            while pieces:
                length = 1
                while length < len(pieces) and pieces[length][0] == sum(pieces[length - 1][:2]):
                    length += 1
                base, end = pieces[0][0], sum(pieces[length - 1][:2])
                span, lanes = pl.ds(base, end - base), pl.ds(start, tile)
                total = jnp.dot(left_high[span, :], right_high[:, lanes], preferred_element_type=jnp.float32)
                total += jnp.dot(left_high[span, :], right_low[:, lanes], preferred_element_type=jnp.float32)
                total += jnp.dot(left_low[span, :], right_high[:, lanes], preferred_element_type=jnp.float32)
                for at, rows, place, out_ref in pieces[:length]:
                    out_ref[place, :, pl.ds(start % width, tile)] = total[at - base : at - base + rows, :]
                pieces = pieces[length:]

    if all(orders[0] == orders[1] for _, _, orders, _ in wanted):
        run(0)
    else:
        for seq in range(2):
            pl.when(here[2] % 2 == seq)(functools.partial(run, seq))


def device_place():
    return [lax.axis_index(name) for name in ("row", "col", "seq")]


def mix_kernel(
    plan, scale, row_blocks, col_blocks, grads, inputs, row_bits, col_bits,
    sent_out, left_high, left_low, right_high, right_low, row_mixed, col_mixed,
    signs, mixing_here,
):
    here = device_place()
    step = pl.program_id(0)
    tokens, row_local = grads.shape
    col_local = inputs.shape[1]

    @pl.when(step == 0)
    def _():
        mixing_here[...] = hadamard_table(CHUNK)
        index = lax.broadcasted_iota(jnp.int32, (1, row_local), 1) + here[0] * row_local
        signs[0:1, :row_local] = jnp.where(index < FF, 1 - 2 * row_bits[...], 0).astype(jnp.float32)
        signs[1:2, :col_local] = (1 - 2 * col_bits[...]).astype(jnp.float32)

    mixing = mixing_here[...]
    row_sign = signs[0:1, :row_local].astype(jnp.bfloat16)
    col_sign = signs[1:2, :col_local].astype(jnp.bfloat16)
    for group in range(row_local // CHUNK // 4):
        parts = []
        for chunk in range(4 * group, 4 * group + 4):
            lanes = slice(chunk * CHUNK, (chunk + 1) * CHUNK)
            signed = grads[:, lanes] * row_sign[:, lanes]
            parts.append(
                lax.dot_general(mixing, signed, (((1,), (1,)), ((), ())), preferred_element_type=jnp.float32)
            )
        for at, part in enumerate(mix_group(parts)):
            row_mixed[4 * group + at] = part
    for group in range(col_local // CHUNK // 4):
        parts = []
        for chunk in range(4 * group, 4 * group + 4):
            lanes = slice(chunk * CHUNK, (chunk + 1) * CHUNK)
            signed = inputs[:, lanes] * col_sign[:, lanes]
            parts.append(jnp.dot(signed, mixing, preferred_element_type=jnp.float32))
        for at, part in enumerate(mix_group(parts)):
            col_mixed[4 * group + at] = part

    now = pl.ds(pl.multiple_of(step * tokens, tokens), tokens)
    row_slots = row_local // BR
    inner = plan.per_row // plan.split
    cut = BR * 3 // 4
    for part in range(plan.split):
        for order, row in enumerate(plan.row_sequence):
            for at in range(inner):
                kept = (here[0] ^ row) * plan.per_row + at * plan.split
                if plan.split == 2:
                    kept = kept + (here[2] ^ part)
                block = row_blocks[kept]
                sign = (1 - 2 * scalar_parity(block // row_slots, here[0])).astype(jnp.float32) * scale
                values = kept_sum(row_mixed, block % row_slots, sign, BR, tokens, 0)
                spot = order * inner + at
                first = plan.first_row(part, 0) + spot * cut
                store_pieces(values[:cut], left_high, left_low, (pl.ds(first, cut), now))
                first = plan.first_row(part, 1) + spot * (BR - cut)
                store_pieces(values[cut:], left_high, left_low, (pl.ds(first, BR - cut), now))
    col_slots = col_local // BC
    for col in range(plan.cols):
        for at in range(plan.per_col):
            block = col_blocks[(here[1] ^ col) * plan.per_col + at]
            sign = (1 - 2 * scalar_parity(block // col_slots, here[1])).astype(jnp.float32)
            values = kept_sum(col_mixed, block % col_slots, sign, BC, tokens, 1)
            store_pieces(values, right_high, right_low, (now, pl.ds((col * plan.per_col + at) * BC, BC)))

    @pl.when(step == pl.num_programs(0) - 1)
    def _():
        factors = (left_high, left_low, right_high, right_low)
        orders = plan.main if plan.split == 1 else plan.main[1:] + plan.main[:1]
        first_row = plan.first_row(plan.split - 1, 0)
        product_blocks(plan, here, factors, [(sent_out, first_row, orders, sent_out.shape[0])])


def product_kernel(plan, wanted, after, left_high, left_low, right_high, right_low, *outs):
    here = device_place()
    factors = (left_high, left_low, right_high, right_low)
    product_blocks(plan, here, factors, [(out, *args) for args, out in zip(wanted, outs)])


def add_kernel(first, second, out):
    out[...] = first[...] + second[...]


def add_early(first, second):
    vmem = pl.BlockSpec(memory_space=pltpu.VMEM)
    return pl.pallas_call(
        add_kernel,
        in_specs=[vmem] * 2,
        out_specs=vmem,
        out_shape=jax.ShapeDtypeStruct(first.shape, first.dtype),
        compiler_params=pltpu.CompilerParams(vmem_limit_bytes=PRODUCT_VMEM),
        cost_estimate=pl.CostEstimate(flops=AHEAD, bytes_accessed=AHEAD // 100, transcendentals=0),
        name="add_early",
    )(first, second)


class Plan:
    def __init__(self, mesh, row_kept, col_kept):
        self.rows, self.cols, self.seqs = mesh.shape["row"], mesh.shape["col"], mesh.shape["seq"]
        self.split = self.seqs if self.seqs == 2 and (row_kept // self.rows) % 2 == 0 else 1
        self.per_row = row_kept // self.rows
        self.per_col = col_kept // self.cols
        low_first = range(self.rows.bit_length() - 2, -1, -1)
        self.row_sequence = [
            sum(((spot >> (self.rows.bit_length() - 2 - bit)) & 1) << bit for bit in low_first) for spot in range(self.rows)
        ]
        row_bits = [("row", 1 << bit) for bit in range(self.rows.bit_length() - 1)]
        col_bits = [("col", 1 << bit) for bit in range(self.cols.bit_length() - 1)]
        last = row_bits[-1:]
        early = col_bits + row_bits[:-1]
        turn = len(early) - 1 if early else 0
        first = early
        second = early[1:] + early[:1]
        third = early[turn:] + early[:turn]
        self.main = (first + last, second + last)
        self.rest = (third + last, third + last)

    def pairs(self, bits):
        found = []
        for row in range(self.rows):
            for col in range(self.cols):
                for seq in range(self.seqs):
                    axis, mask = bits[seq % 2]
                    other_row = row ^ mask if axis == "row" else row
                    other_col = col ^ mask if axis == "col" else col
                    found.append(
                        (
                            (row * self.cols + col) * self.seqs + seq,
                            (other_row * self.cols + other_col) * self.seqs + seq,
                        )
                    )
        return found

    def place(self, order, row, col):
        spot = 0
        for axis, mask in order:
            spot = spot * 2 + int(bool((row if axis == "row" else col) & mask))
        return spot

    def first_row(self, part, kind):
        inner = self.per_row // self.split * self.rows
        main, rest = inner * (BR * 3 // 4), inner * (BR - BR * 3 // 4)
        if self.split == 1:
            return (0, main)[kind]
        return ((0, main + rest), (main + 2 * rest, main))[part][kind]

    def cross(self, part, orders, step):
        bits = (orders[0][step], orders[1][step])
        return lax.ppermute(part, ("row", "col", "seq"), self.pairs(bits))

    def halve(self, part, orders, step):
        half = part.shape[0] // 2
        return part[:half] + self.cross(part[half:], orders, step)


def body(plan, out_grads, layer_inputs, row_bits, col_bits, row_blocks, col_blocks):
    tokens, row_local = out_grads.shape[1:]
    col_local = layer_inputs.shape[2]
    tile = min(TILE, tokens)
    start = jnp.zeros((8, 128), jnp.float32)
    scale = 1.0 / math.sqrt(row_local * plan.rows * col_local * plan.cols)
    left_rows = plan.rows * plan.per_row * BR
    right_cols = plan.cols * plan.per_col * BC
    inner = plan.per_row // plan.split
    cut = BR * 3 // 4
    cols_each = plan.per_col * BC
    blocks = plan.rows * plan.cols
    smem = pl.BlockSpec(memory_space=pltpu.SMEM)
    vmem = pl.BlockSpec(memory_space=pltpu.VMEM)
    main_shape = jax.ShapeDtypeStruct((blocks // 2, inner * cut, cols_each), jnp.float32)
    rest_shape = jax.ShapeDtypeStruct((blocks, inner * (BR - cut), cols_each), jnp.float32)
    first_sent, *factors = pl.pallas_call(
        functools.partial(mix_kernel, plan, scale),
        grid=(tokens // tile,),
        in_specs=[
            smem,
            smem,
            pl.BlockSpec((tile, row_local), lambda step: (step, 0)),
            pl.BlockSpec((tile, col_local), lambda step: (step, 0)),
            pl.BlockSpec((1, row_local), lambda step: (0, 0)),
            pl.BlockSpec((1, col_local), lambda step: (0, 0)),
        ],
        out_specs=[vmem] * 5,
        out_shape=[
            main_shape,
            pltpu.VMEM((left_rows, tokens), jnp.bfloat16),
            pltpu.VMEM((left_rows, tokens), jnp.bfloat16),
            pltpu.VMEM((tokens, right_cols), jnp.bfloat16),
            pltpu.VMEM((tokens, right_cols), jnp.bfloat16),
        ],
        scratch_shapes=[
            pltpu.VMEM((row_local // CHUNK, CHUNK, tile), jnp.float32),
            pltpu.VMEM((col_local // CHUNK, tile, CHUNK), jnp.float32),
            pltpu.VMEM((8, max(row_local, col_local)), jnp.float32),
            pltpu.VMEM((CHUNK, CHUNK), jnp.bfloat16),
        ],
        compiler_params=pltpu.CompilerParams(vmem_limit_bytes=MIX_VMEM),
        name="mix",
    )(
        pltpu.with_memory_space_constraint(row_blocks, pltpu.HBM),
        pltpu.with_memory_space_constraint(col_blocks, pltpu.HBM),
        *(pltpu.with_memory_space_constraint(array, pltpu.HBM) for array in (out_grads[0], layer_inputs[0])),
        *(pltpu.with_memory_space_constraint(bits[None], pltpu.HBM) for bits in (row_bits, col_bits)),
    )

    def products(wanted, shapes, name, after=start):
        return pl.pallas_call(
            functools.partial(product_kernel, plan, wanted),
            in_specs=[pl.BlockSpec(memory_space=pl.ANY)] + [vmem] * 4,
            out_specs=[vmem] * len(shapes),
            out_shape=shapes,
            compiler_params=pltpu.CompilerParams(vmem_limit_bytes=PRODUCT_VMEM),
            name=name,
        )(after, *factors)

    half = blocks // 2

    def swap(values):
        return lax.ppermute(values, "seq", [(0, 1), (1, 0)])

    if plan.split == 2:
        arrived_sent = swap(first_sent)
        sent, rest_other = products(
            [(0, plan.main, half), (plan.first_row(1, 1), plan.rest, 0)], [main_shape, rest_shape], "sent_products"
        )
        sent = sent + arrived_sent
        later, sent = lax.optimization_barrier((start, sent))
        after, arrived_rest = lax.optimization_barrier((later, swap(rest_other)))
        (rest,) = products([(plan.first_row(0, 1), plan.rest, 0)], [rest_shape], "rest_product", after)
        rest = rest + arrived_rest
        (kept_other,) = products([(plan.first_row(1, 0), plan.main[1:] + plan.main[:1], 0)], [main_shape], "kept_other_product", later)
        (kept,) = products([(0, plan.main, 0)], [main_shape], "kept_product", later)
        main = add_early(kept, plan.cross(sent, plan.main, 0)) + swap(kept_other)
    else:
        (rest,) = products([(plan.first_row(0, 1), plan.rest, 0)], [rest_shape], "rest_product")
        (kept,) = products([(0, plan.main, 0)], [main_shape], "kept_product")
        main = kept + plan.cross(first_sent, plan.main, 0)
    steps = len(plan.main[0])
    rest = plan.halve(rest, plan.rest, 0)
    for step in range(1, steps - 1):
        main = plan.halve(main, plan.main, step)
        arrived = plan.cross(rest[rest.shape[0] // 2 :], plan.rest, step)
        main, arrived = lax.optimization_barrier((main, arrived))
        rest = rest[: rest.shape[0] // 2] + arrived
    both = plan.halve(jnp.concatenate([main, rest], axis=1), plan.rest, steps - 1)[0]

    def in_rows(values):
        first = values[: inner * cut].reshape(inner, cut, cols_each)
        second = values[inner * cut :].reshape(inner, BR - cut, cols_each)
        return jnp.concatenate([first, second], axis=1)

    if plan.split == 2:
        mine, other = in_rows(both), in_rows(swap(both))
        first = lax.axis_index("seq") == 0
        pair = jnp.stack([jnp.where(first, mine, other), jnp.where(first, other, mine)], axis=1)
        return pair.reshape(1, plan.per_row * BR, cols_each)
    return in_rows(lax.psum(both, "seq")).reshape(1, plan.per_row * BR, cols_each)


def solution(mesh):
    def run(out_grads, layer_inputs, row_bits, col_bits, row_blocks, col_blocks):
        plan = Plan(mesh, row_blocks.shape[0], col_blocks.shape[0])
        in_specs = (P(None, "seq", "row"), P(None, "seq", "col"), P("row"), P("col"), P(), P())
        return jax.shard_map(
            lambda *args: body(plan, *args),
            mesh=mesh,
            in_specs=in_specs,
            out_specs=P(None, "row", "col"),
            check_vma=False,
        )(out_grads, layer_inputs, row_bits, col_bits, row_blocks, col_blocks)

    return run
```
